32 devices in a mesh: section: 2 (over x), dp: 16 (over z, y, core).
Axes of the slice: x: 2, y: 2, z: 4, core: 2. Of those that a mesh axis runs over, the one named last changes fastest.
Arguments:
- incoming: bfloat16 [2, 4, 2048, 256], P('section', None, 'dp'), may hold values from -6 to 6
- feed: bfloat16 [4, 4, 2048, 256], P(None, None, 'dp'), may hold values from -6 to 6
- plan: int32 [1, 16], P(None, 'dp'), may hold values from 0 to 3, as said below
- weights: bfloat16 [2, 2, 27, 256, 256], P('section'), may hold values from -0.078125 to 0.078125
- momentum: float32 [2, 2, 27, 256, 256], P('section', None, None, 'dp'), may hold values from -6 to 6
Outputs:
- upstream: bfloat16 [2, 2, 4, 2048, 256], P(None, 'section', None, 'dp')
- new_momentum: float32 [2, 2, 27, 256, 256], P('section', None, None, 'dp')
The draws below stay inside these ranges and needn't reach their ends.
Inputs may be any that keep to these rules, and one draw needn't show every extreme that they name: `plan`: every micro-batch of the pool is taken by some tile in some tick.
All inputs are finite; a program needn't handle non-finite values.
Results may differ from the reference program's by a relative error of at most 0.014.
Values may be sent and summed in bfloat16 or wider, within the bound.
A program may use at most 128 MiB of HBM per device.

```python
import jax
import jax.numpy as jnp
from jax import lax

C = 256
TD = 2
TH = 8
TW = 8
TICKS = 2
POOL = 4
VOX = 128
VOX_ALL = 2048
N_SECTION = 2
N_DP = 16


def draw_plan(key, part):
    count = (TICKS - 1) * N_DP
    order = jax.random.permutation(key, count)
    return (order % POOL).reshape(TICKS - 1, N_DP).astype(jnp.int32)


def with_spikes(values, rng, source, target, blocks, factor):
    def block_of(position):
        return (jnp.arange(values.shape[position]) // (values.shape[position] // blocks)).reshape((-1,) + (1,) * (values.ndim - 1 - position))

    first = jax.random.permutation(rng, blocks)[block_of(target)]
    second = (block_of(target) + blocks // 2) % blocks
    return jnp.where((block_of(source) == first) | (block_of(source) == second), factor * values, values)


def block_scale(stream_key, shape, cuts, low, top_value):
    gain, own = 1.0, jax.random.fold_in(stream_key, 6)
    for position, parts in cuts:
        steps = jnp.exp(jax.random.uniform(jax.random.fold_in(own, position), (parts,), jnp.float32, low / len(cuts), top_value / len(cuts)))
        gain = gain * jnp.repeat(steps, shape[position] // parts).reshape([-1 if axis == position else 1 for axis in range(len(shape))])
    return gain


def normal_values(own_key, shape, deviation, reach, cuts=(), dtype=jnp.bfloat16):
    drawn = jax.random.normal(own_key, shape, jnp.float32) * deviation
    if len(cuts) > 0:
        drawn = block_scale(own_key, shape, cuts, -0.22, 0.18) * drawn
    return jnp.clip(drawn, min=-reach, max=reach).astype(dtype)


def noise_with(rng, extent, scale, reach, cuts, heavy, kind=jnp.bfloat16):
    drawn = scale * jax.random.normal(rng, extent, jnp.float32)
    if cuts:
        drawn = drawn * block_scale(rng, extent, cuts, -0.22, 0.18)
    return jnp.clip(with_spikes(drawn, jax.random.fold_in(rng, 3), *heavy), -reach, reach).astype(kind)


def setup_inputs(seed: int = 0) -> dict:
    seeds = jax.random.split(jax.random.key(seed), 6)
    incoming = noise_with(seeds[0], (N_SECTION, 4, VOX_ALL, C), 1.0, 6.0, ((0, 2), (2, 16)), (2, 3, 16, 2.0))
    feed = normal_values(seeds[1], (POOL, 4, VOX_ALL, C), 1.0, 6.0, ((2, 16),))
    plan = draw_plan(jax.random.fold_in(seeds[5], 71), 0)
    weights = normal_values(seeds[3], (N_SECTION, 2, 27, C, C), (27 * C) ** -0.5, 0.078125, ((0, 2),))
    momentum = normal_values(seeds[4], (N_SECTION, 2, 27, C, C), 1.0, 6.0, ((0, 2), (3, 16)), jnp.float32)
    return {"incoming": incoming, "feed": feed, "plan": plan, "weights": weights, "momentum": momentum}


def make_patches(act, sign):
    volume = act.reshape(TD, TH, TW, act.shape[-1])
    padded = jnp.pad(volume, ((1, 1), (1, 1), (1, 1), (0, 0)))
    pieces = []
    for depth in (-1, 0, 1):
        for height in (-1, 0, 1):
            for width in (-1, 0, 1):
                start_d = 1 + sign * depth
                start_h = 1 + sign * height
                start_w = 1 + sign * width
                cut = padded[start_d:start_d + TD, start_h:start_h + TH, start_w:start_w + TW]
                pieces.append(cut.reshape(VOX, act.shape[-1]))
    return jnp.stack(pieces, axis=1)

def silu_grad(value):
    sig = jax.nn.sigmoid(value)
    return sig * (1.0 + value * (1.0 - sig))

def tile_back(inputs, weight):
    y_one = inputs[0]
    y_two = inputs[1]
    dy_one = inputs[2].astype(jnp.float32)
    dy_two = inputs[3]
    weight_f = weight[0].astype(jnp.float32)
    weight_g = weight[1].astype(jnp.float32)
    y_one_f = y_one.astype(jnp.float32)
    act_one = jax.nn.silu(y_one_f).astype(jnp.bfloat16)
    patch_one = make_patches(act_one, 1).astype(jnp.float32)
    g_out = jnp.einsum('vtc,toc->vo', patch_one, weight_g)
    x_two = (y_two.astype(jnp.float32) - g_out).astype(jnp.bfloat16)
    grad_g = jnp.einsum('vo,vti->toi', dy_two.astype(jnp.float32), patch_one)
    back_two = make_patches(dy_two, -1).astype(jnp.float32)
    d_act_one = jnp.einsum('vto,toi->vi', back_two, weight_g)
    dx_one = (dy_one + d_act_one * silu_grad(y_one_f)).astype(jnp.bfloat16)
    x_two_f = x_two.astype(jnp.float32)
    act_two = jax.nn.silu(x_two_f).astype(jnp.bfloat16)
    patch_two = make_patches(act_two, 1).astype(jnp.float32)
    f_out = jnp.einsum('vtc,toc->vo', patch_two, weight_f)
    x_one = (y_one_f - f_out).astype(jnp.bfloat16)
    grad_f = jnp.einsum('vo,vti->toi', dx_one.astype(jnp.float32), patch_two)
    back_one = make_patches(dx_one, -1).astype(jnp.float32)
    d_act_two = jnp.einsum('vto,toi->vi', back_one, weight_f)
    dx_two = (dy_two.astype(jnp.float32) + d_act_two * silu_grad(x_two_f)).astype(jnp.bfloat16)
    return (jnp.stack([x_one, x_two, dx_one, dx_two]), jnp.stack([grad_f, grad_g]))

def section_outs(pair):
    inputs, weight = pair
    tiles = inputs.reshape(4, N_DP, VOX, C)

    def one_tile(carry, index):
        outs, grads = tile_back(tiles[:, index], weight)
        return (carry, outs)
    unused, outs = lax.scan(one_tile, jnp.zeros((), jnp.float32), jnp.arange(N_DP))
    return jnp.transpose(outs, (1, 0, 2, 3)).reshape(4, VOX_ALL, C)

def section_grads(pair):
    seen, weight = pair
    tiles = seen.reshape(TICKS, 4, N_DP, VOX, C)

    def one_tile(carry, index):
        term = jnp.zeros((2, 27, C, C), jnp.float32)
        for tick in range(TICKS):
            outs, grads = tile_back(tiles[tick, :, index], weight)
            term = term + grads
        part = term.astype(jnp.bfloat16).astype(jnp.float32)
        return (carry + part, None)
    zero = jnp.zeros((2, 27, C, C), jnp.float32)
    total, unused = lax.scan(one_tile, zero, jnp.arange(N_DP))
    return total

def reference(incoming, feed, plan, weights, momentum):
    current = incoming
    results = []
    seen = []
    for tick in range(TICKS):
        seen.append(current)
        outs = lax.map(section_outs, (current, weights))
        results.append(outs)
        if tick + 1 < TICKS:
            pool = feed.reshape(POOL, 4, N_DP, VOX, C)
            picks = plan[tick]
            chosen = pool[picks, :, jnp.arange(N_DP)]
            chosen = jnp.transpose(chosen, (1, 0, 2, 3)).reshape(4, VOX_ALL, C)
            current = jnp.concatenate([outs[1:], chosen[None]], axis=0)
    seen_all = jnp.stack(seen, axis=1)
    grad_total = lax.map(section_grads, (seen_all, weights))
    upstream = jnp.stack(results)
    new_momentum = 0.9 * momentum + grad_total / (N_DP * TICKS)
    return (upstream, new_momentum)
```

```python
import functools

import jax
import jax.numpy as jnp
from jax import lax
from jax.experimental import pallas as pl
from jax.experimental.pallas import tpu as pltpu
from jax.sharding import PartitionSpec as P

TD = 2
TH = 8
TW = 8
TICKS = 2
VOX = TD * TH * TW
PLANE = TH * TW
TAPS = 27
LANES = 128
MESH = pl.DeviceIdType.MESH


def tap_offset(tap):
    return tap // 9 - 1, (tap // 3) % 3 - 1, tap % 3 - 1


def sigmoid(u):
    return 1.0 / (1.0 + jnp.exp(-u))


def silu_grad(u, s):
    return s * (1.0 + u * (1.0 - s))


def fill(even, odd, x):
    row = lax.broadcasted_iota(jnp.int32, x.shape, 0)
    w = row % TW
    edge = jnp.zeros((TW, x.shape[1]), jnp.float32)
    for wi, dw in enumerate((-1, 0, 1)):
        s = x
        if dw:
            s = pltpu.roll(x, (-dw) % VOX, 0)
            s = jnp.where((w + dw >= 0) & (w + dw < TW), s, 0.0)
        for d in range(TD):
            plane = s[d * PLANE:(d + 1) * PLANE]
            odd[wi, d + 1] = plane.astype(jnp.bfloat16)
            even[wi, d + 1] = jnp.concatenate([edge, plane, edge], 0).astype(jnp.bfloat16)


def patch(even, odd, tap):
    dd, dh, dw = tap_offset(tap)
    if dh == 0:
        cut = odd[dw + 1, dd + 1:dd + 1 + TD]
    else:
        lo = (dh + 1) * TW
        cut = even[dw + 1, dd + 1:dd + 1 + TD, lo:lo + PLANE]
    return cut.reshape(VOX, cut.shape[-1])


def kernel(n, nsec, plan, incoming, feed, weights, up, grad,
           w_ref, nxt, ea, oa, eb, ob, a_send, d_send, a_recv, d_recv, big, acc, g_send, g_recv,
           w_sem, sec_s, sec_r, as_s, as_r, ds_s, ds_r, g_s, g_r):
    me = lax.axis_index("dp")
    sec = lax.axis_index("section")
    core = lax.rem(me, 2)
    chip = me // 2
    mate = me + 1 - 2 * core
    block = d_recv.shape[2]
    half = block // 2
    last = sec == nsec - 1
    loads = [pltpu.make_async_copy(weights.at[0, b], w_ref.at[b], w_sem.at[b]) for b in (0, 1)]
    loads[1].start()
    loads[0].start()

    barrier = pltpu.get_barrier_semaphore()

    @pl.loop(1, n)
    def _(k):
        pl.semaphore_signal(barrier, inc=1, device_id={"dp": lax.rem(me + k, n)}, device_id_type=MESH)

    @pl.when(sec > 0)
    def _():
        pl.semaphore_signal(barrier, inc=1, device_id={"section": sec - 1}, device_id_type=MESH)

    @pl.when(sec < nsec - 1)
    def _():
        pl.semaphore_signal(barrier, inc=1, device_id={"section": sec + 1}, device_id_type=MESH)

    for wi in range(3):
        for ref in (ea, oa, eb, ob):
            for d in (0, TD + 1):
                ref[wi, d] = jnp.zeros(ref.shape[2:], jnp.bfloat16)

    @pl.when(last)
    def _():
        nxt[...] = feed[plan[0, 0]]

    extra = jnp.where(sec > 0, 1, 0) + jnp.where(sec < nsec - 1, 1, 0)
    pl.semaphore_wait(barrier, n - 1 + extra)

    def a_copy(stage, peer, slot):
        return pltpu.make_async_remote_copy(
            src_ref=a_send.at[stage, lax.rem(peer, 2)], dst_ref=a_recv.at[stage, slot],
            send_sem=as_s.at[stage, peer], recv_sem=as_r.at[stage, slot],
            device_id={"dp": peer}, device_id_type=MESH)

    def d_copy(stage, peer, slot):
        return pltpu.make_async_remote_copy(
            src_ref=d_send.at[stage, peer // 2], dst_ref=d_recv.at[stage, slot],
            send_sem=ds_s.at[stage, peer], recv_sem=ds_r.at[stage, slot],
            device_id={"dp": peer}, device_id_type=MESH)

    def share(stage, act, err):
        a_send[stage, 0] = act[:, :LANES]
        a_send[stage, 1] = act[:, LANES:]
        turned = jnp.transpose(err).astype(jnp.bfloat16)
        d_send[stage] = turned.reshape(d_send.shape[1:])
        a_recv[stage, me] = a_send[stage, core]
        d_recv[stage, me] = d_send[stage, chip]

        @pl.loop(1, n)
        def _(k):
            peer = lax.rem(me + k, n)
            d_copy(stage, peer, me).start()
            a_copy(stage, peer, me).start()

    def convs(b):
        fwd = jnp.zeros((VOX, w_ref.shape[2]), jnp.float32)
        for tap in range(TAPS):
            fwd += lax.dot_general(patch(ea, oa, tap), w_ref[b, tap], (((1,), (1,)), ((), ())),
                                   preferred_element_type=jnp.float32)
        bwd = jnp.zeros((VOX, w_ref.shape[3]), jnp.float32)
        for tap in range(TAPS):
            bwd += jnp.dot(patch(eb, ob, TAPS - 1 - tap), w_ref[b, tap],
                           preferred_element_type=jnp.float32)
        return fwd, bwd

    def sec_copy(j):
        return pltpu.make_async_remote_copy(
            src_ref=up.at[0, j], dst_ref=nxt.at[j], send_sem=sec_s.at[j], recv_sem=sec_r.at[j],
            device_id={"section": lax.rem(sec + nsec - 1, nsec)}, device_id_type=MESH)

    for tick in range(TICKS):
        if tick == 0:
            cur = incoming.at[0]
        else:
            cur = nxt

            @pl.when(sec < nsec - 1)
            def _():
                for j in range(4):
                    sec_copy(j).wait_recv()
        y1 = cur[0].astype(jnp.float32)
        s1 = sigmoid(y1)
        a1 = y1 * s1
        dy2 = cur[3].astype(jnp.float32)
        share(2 * tick, a1.astype(jnp.bfloat16), dy2)
        fill(ea, oa, a1)
        fill(eb, ob, dy2)
        if tick == 0:
            loads[1].wait()
        fwd, bwd = convs(1)
        x2 = (cur[1].astype(jnp.float32) - fwd).astype(jnp.bfloat16)
        dx1 = (cur[2].astype(jnp.float32) + bwd * silu_grad(y1, s1)).astype(jnp.bfloat16)
        up[tick, 1] = x2
        up[tick, 2] = dx1
        if tick == 0:
            @pl.when(sec > 0)
            def _():
                sec_copy(1).start()
                sec_copy(2).start()
        u = x2.astype(jnp.float32)
        s2 = sigmoid(u)
        a2 = u * s2
        e1 = dx1.astype(jnp.float32)
        share(2 * tick + 1, a2.astype(jnp.bfloat16), e1)
        fill(ea, oa, a2)
        fill(eb, ob, e1)
        if tick == 0:
            loads[0].wait()
        fwd, bwd = convs(0)
        u = up[tick, 1].astype(jnp.float32)
        s2 = sigmoid(u)
        up[tick, 0] = (cur[0].astype(jnp.float32) - fwd).astype(jnp.bfloat16)
        up[tick, 3] = (cur[3].astype(jnp.float32) + bwd * silu_grad(u, s2)).astype(jnp.bfloat16)
        if tick == 0:
            @pl.when(sec > 0)
            def _():
                sec_copy(0).start()
                sec_copy(3).start()

    lane = lax.broadcasted_iota(jnp.int32, (block, VOX), 1)
    ld, lh, lw = lane // PLANE, (lane // TW) % TH, lane % TW

    def g_copy(b):
        return pltpu.make_async_remote_copy(
            src_ref=g_send.at[b], dst_ref=g_recv.at[b], send_sem=g_s.at[b], recv_sem=g_r.at[b],
            device_id={"dp": mate}, device_id_type=MESH)

    tiles = 3
    per = TAPS * block // tiles
    for stage in range(2 * TICKS):
        b = stage % 2

        @pl.loop(1, n)
        def _(k):
            peer = lax.rem(me + k, n)
            d_copy(stage, me, peer).wait_recv()
            a_copy(stage, me, peer).wait_recv()

        @pl.loop(0, n)
        def _(r):
            x = d_recv[stage, r].astype(jnp.float32)
            cols = pl.ds(pl.multiple_of(r * VOX, VOX), VOX)
            for tap in range(TAPS):
                dd, dh, dw = tap_offset(tap)
                flat = dd * PLANE + dh * TW + dw
                s = x if flat == 0 else pltpu.roll(x, flat % VOX, 1)
                ok = None
                for c, by, size in ((ld, dd, TD), (lh, dh, TH), (lw, dw, TW)):
                    if by:
                        this = c >= 1 if by > 0 else c < size - 1
                        ok = this if ok is None else ok & this
                if ok is not None:
                    s = jnp.where(ok, s, 0.0)
                big[tap * block:(tap + 1) * block, cols] = s.astype(jnp.bfloat16)

        @pl.loop(0, tiles)
        def _(m):
            rows = pl.ds(pl.multiple_of(m * per, 16), per)
            got = jnp.dot(big[rows, :], a_recv[stage].reshape(n * VOX, LANES),
                          preferred_element_type=jnp.float32)
            if stage < 2:
                acc[b, rows, :] = got
            else:
                acc[b, rows, :] += got
        if stage >= 2 * TICKS - 2:
            view = acc.at[b]
            for tap in range(TAPS):
                lo = pl.multiple_of(tap * block + (1 - core) * half, 8)
                g_send[b, tap] = view[pl.ds(lo, half), :]
            g_copy(b).start()
    mine = pl.ds(pl.multiple_of(core * LANES, LANES), LANES)
    other = pl.ds(pl.multiple_of((1 - core) * LANES, LANES), LANES)
    for b in (0, 1):
        for tap in range(TAPS):
            lo = pl.multiple_of(tap * block + core * half, 8)
            grad[1 - b, tap, :, mine] = acc[b, pl.ds(lo, half), :]
    for b in (0, 1):
        g_copy(b).wait_recv()
        grad[1 - b, :, :, other] = g_recv[b]
    for b in (0, 1):
        g_copy(b).wait_send()
    for stage in range(2 * TICKS):
        @pl.loop(1, n)
        def _(k):
            peer = lax.rem(me + k, n)
            d_copy(stage, peer, me).wait_send()
            a_copy(stage, peer, me).wait_send()

    @pl.when(sec > 0)
    def _():
        for j in range(4):
            sec_copy(j).wait_send()


def body(incoming, feed, plan, weights, momentum):
    n = lax.axis_size("dp")
    nsec = lax.axis_size("section")
    channels = weights.shape[-1]
    block = 2 * channels // n
    stages = 2 * TICKS
    bf, f32 = jnp.bfloat16, jnp.float32
    vm = pl.BlockSpec(memory_space=pltpu.VMEM)
    dma = pltpu.SemaphoreType.DMA
    up, grad = pl.pallas_call(
        functools.partial(kernel, n, nsec),
        out_shape=(
            jax.ShapeDtypeStruct((TICKS, 4, VOX, channels), bf),
            jax.ShapeDtypeStruct((2, TAPS, block // 2, channels), f32),
        ),
        in_specs=[pl.BlockSpec(memory_space=pltpu.SMEM), vm, vm, pl.BlockSpec(memory_space=pl.ANY)],
        out_specs=(vm, vm),
        scratch_shapes=[
            pltpu.VMEM(weights.shape[1:], bf),
            pltpu.VMEM((4, VOX, channels), bf),
            pltpu.VMEM((3, TD + 2, PLANE + 2 * TW, channels), bf),
            pltpu.VMEM((3, TD + 2, PLANE, channels), bf),
            pltpu.VMEM((3, TD + 2, PLANE + 2 * TW, channels), bf),
            pltpu.VMEM((3, TD + 2, PLANE, channels), bf),
            pltpu.VMEM((stages, 2, VOX, LANES), bf),
            pltpu.VMEM((stages, n // 2, block, VOX), bf),
            pltpu.VMEM((stages, n, VOX, LANES), bf),
            pltpu.VMEM((stages, n, block, VOX), bf),
            pltpu.VMEM((TAPS * block, n * VOX), bf),
            pltpu.VMEM((2, TAPS * block, LANES), f32),
            pltpu.VMEM((2, TAPS, block // 2, LANES), f32),
            pltpu.VMEM((2, TAPS, block // 2, LANES), f32),
            dma((2,)), dma((4,)), dma((4,)),
            dma((stages, n)), dma((stages, n)), dma((stages, n)), dma((stages, n)),
            dma((2,)), dma((2,)),
        ],
        compiler_params=pltpu.CompilerParams(
            collective_id=0, has_side_effects=True, vmem_limit_bytes=48 * 1024 * 1024),
        cost_estimate=pl.CostEstimate(flops=12 * TICKS * VOX * TAPS * channels * channels,
                                      bytes_accessed=weights.size * 2, transcendentals=0),
    )(plan, incoming, feed, weights)
    new_momentum = 0.9 * momentum[0] + grad / (n * TICKS)
    return (up[:, None], new_momentum[None])


def solution(mesh):
    in_specs = (
        P("section", None, "dp", None),
        P(None, None, "dp", None),
        P(None, "dp"),
        P("section", None, None, None, None),
        P("section", None, None, "dp", None),
    )
    out_specs = (P(None, "section", None, "dp", None), P("section", None, None, "dp", None))
    return jax.shard_map(body, mesh=mesh, in_specs=in_specs, out_specs=out_specs, check_vma=False)
```

```python
import functools

import jax
import jax.numpy as jnp
from jax import lax
from jax.experimental import pallas as pl
from jax.experimental.pallas import tpu as pltpu
from jax.sharding import PartitionSpec as P

TD = 2
TH = 8
TW = 8
TICKS = 2
VOX = TD * TH * TW
PLANE = TH * TW
TAPS = 27
LANES = 128
MESH = pl.DeviceIdType.MESH


def tap_offset(tap):
    return tap // 9 - 1, (tap // 3) % 3 - 1, tap % 3 - 1


def sigmoid(u):
    return 1.0 / (1.0 + jnp.exp(-u))


def silu_grad(u, s):
    return s * (1.0 + u * (1.0 - s))


def fill(even, odd, x):
    row = lax.broadcasted_iota(jnp.int32, x.shape, 0)
    w = row % TW
    edge = jnp.zeros((TW, x.shape[1]), jnp.float32)
    for wi, dw in enumerate((-1, 0, 1)):
        s = x
        if dw:
            s = pltpu.roll(x, (-dw) % VOX, 0)
            s = jnp.where((w + dw >= 0) & (w + dw < TW), s, 0.0)
        for d in range(TD):
            plane = s[d * PLANE:(d + 1) * PLANE]
            odd[wi, d + 1] = plane.astype(jnp.bfloat16)
            even[wi, d + 1] = jnp.concatenate([edge, plane, edge], 0).astype(jnp.bfloat16)


def patch(even, odd, tap):
    dd, dh, dw = tap_offset(tap)
    if dh == 0:
        cut = odd[dw + 1, dd + 1:dd + 1 + TD]
    else:
        lo = (dh + 1) * TW
        cut = even[dw + 1, dd + 1:dd + 1 + TD, lo:lo + PLANE]
    return cut.reshape(VOX, cut.shape[-1])


def kernel(n, nsec, plan, incoming, feed, weights, up, grad,
           w_ref, first, pool, nxt, upv, ea, oa, eb, ob, a_send, d_send, d_mid, a_recv, d_recv, big, acc,
           g_send, g_recv, w_sem, in_sem, up_sem, sec_s, sec_r, as_s, as_r, ar_s, ar_r,
           dz_s, dz_r, dy_s, dy_r, dm_s, dm_r, g_s, g_r):
    me = lax.axis_index("dp")
    sec = lax.axis_index("section")
    ny, nz = a_recv.shape[1:3]
    core = lax.rem(me, 2)
    y = lax.rem(me // 2, ny)
    z = me // (2 * ny)
    mate = me + 1 - 2 * core
    block = d_recv.shape[-2]
    half = block // 2
    last = sec == nsec - 1

    def at(zz, yy, cc):
        return (zz * ny + yy) * 2 + cc

    def z_of(k):
        return lax.rem(z + k, nz)

    def y_of(k):
        return lax.rem(y + k, ny)

    load_in = pltpu.make_async_copy(incoming.at[0], first, in_sem.at[0])
    load_pool = pltpu.make_async_copy(feed, pool, in_sem.at[1])
    loads = [pltpu.make_async_copy(weights.at[0, b], w_ref.at[b], w_sem.at[b]) for b in (0, 1)]
    load_in.start()
    loads[1].start()
    loads[0].start()
    load_pool.start()

    barrier = pltpu.get_barrier_semaphore()
    peers = [mate]
    peers += [at(z_of(k), y, cc) for k in range(1, nz) for cc in (0, 1)]
    peers += [at(z, y_of(k), cc) for k in range(1, ny) for cc in (0, 1)]
    for peer in peers:
        pl.semaphore_signal(barrier, inc=1, device_id={"dp": peer}, device_id_type=MESH)

    @pl.when(sec > 0)
    def _():
        pl.semaphore_signal(barrier, inc=1, device_id={"section": sec - 1}, device_id_type=MESH)

    @pl.when(sec < nsec - 1)
    def _():
        pl.semaphore_signal(barrier, inc=1, device_id={"section": sec + 1}, device_id_type=MESH)

    for wi in range(3):
        for ref in (ea, oa, eb, ob):
            for d in (0, TD + 1):
                ref[wi, d] = jnp.zeros(ref.shape[2:], jnp.bfloat16)
    load_in.wait()
    extra = jnp.where(sec > 0, 1, 0) + jnp.where(sec < nsec - 1, 1, 0)
    pl.semaphore_wait(barrier, len(peers) + extra)

    def a_direct(stage, idx, peer, to, slot):
        return pltpu.make_async_remote_copy(
            src_ref=a_send.at[stage, to], dst_ref=a_recv.at[(stage,) + slot],
            send_sem=as_s.at[stage, idx], recv_sem=as_r.at[(stage,) + slot],
            device_id={"dp": peer}, device_id_type=MESH)

    def a_relay(stage, yy, slot):
        return pltpu.make_async_remote_copy(
            src_ref=a_recv.at[(stage,) + slot], dst_ref=a_recv.at[(stage,) + slot],
            send_sem=ar_s.at[stage, yy, slot[1]], recv_sem=ar_r.at[(stage,) + slot],
            device_id={"dp": at(z, yy, core)}, device_id_type=MESH)

    def d_along_z(stage, zz, slot):
        return pltpu.make_async_remote_copy(
            src_ref=d_send.at[stage, zz], dst_ref=d_mid.at[stage, :, slot],
            send_sem=dz_s.at[stage, zz], recv_sem=dz_r.at[stage, slot],
            device_id={"dp": at(zz, y, core)}, device_id_type=MESH)

    def d_along_y(stage, yy, slot):
        return pltpu.make_async_remote_copy(
            src_ref=d_mid.at[stage, yy], dst_ref=d_recv.at[stage, core, slot],
            send_sem=dy_s.at[stage, yy], recv_sem=dy_r.at[stage, slot],
            device_id={"dp": at(z, yy, core)}, device_id_type=MESH)

    def d_to_mate(stage, whose):
        return pltpu.make_async_remote_copy(
            src_ref=d_recv.at[stage, whose], dst_ref=d_recv.at[stage, whose],
            send_sem=dm_s.at[stage], recv_sem=dm_r.at[stage],
            device_id={"dp": mate}, device_id_type=MESH)

    def directs(stage):
        mine = (y, z, core)
        out = []
        for k in range(1, nz):
            for cc in (0, 1):
                out.append(a_direct(stage, len(out), at(z_of(k), y, cc), cc, mine))
        for k in range(1, ny):
            for cc in (0, 1):
                out.append(a_direct(stage, len(out), at(z, y_of(k), cc), cc, mine))
        out.append(a_direct(stage, len(out), mate, 1 - core, mine))
        return out

    def share(stage, act, err):
        a_send[stage, 0] = act[:, :LANES]
        a_send[stage, 1] = act[:, LANES:]
        turned = jnp.transpose(err).astype(jnp.bfloat16)
        d_send[stage] = turned.reshape(d_send.shape[1:])
        for k in range(1, nz):
            d_along_z(stage, z_of(k), z).start()
        for copy in directs(stage):
            copy.start()
        a_recv[stage, y, z, core] = a_send[stage, core]
        for yy in range(ny):
            d_mid[stage, yy, z] = d_send[stage, z, yy]

    def relay(stage):
        for k in range(1, nz):
            d_along_z(stage, z, z_of(k)).wait_recv()
        for k in range(1, ny):
            d_along_y(stage, y_of(k), y).start()
        d_recv[stage, core, y] = d_mid[stage, y]
        for k in range(1, nz):
            for cc in (0, 1):
                a_direct(stage, 0, mate, 0, (y, z_of(k), cc)).wait_recv()
            for j in range(1, ny):
                a_relay(stage, y_of(j), (y, z_of(k))).start()

    def swap_errors(stage):
        for k in range(1, ny):
            d_along_y(stage, y, y_of(k)).wait_recv()
        d_to_mate(stage, core).start()

    def arrive(stage):
        a_direct(stage, 0, mate, 0, (y, z, 1 - core)).wait_recv()
        for j in range(1, ny):
            for cc in (0, 1):
                a_direct(stage, 0, mate, 0, (y_of(j), z, cc)).wait_recv()
            for k in range(1, nz):
                a_relay(stage, y, (y_of(j), z_of(k))).wait_recv()

    def sent(stage):
        for k in range(1, nz):
            d_along_z(stage, z_of(k), z).wait_send()
        for copy in directs(stage):
            copy.wait_send()
        for j in range(1, ny):
            d_along_y(stage, y_of(j), y).wait_send()
            for k in range(1, nz):
                a_relay(stage, y_of(j), (y, z_of(k))).wait_send()
        d_to_mate(stage, core).wait_send()

    def convs(b, hook):
        fwd = jnp.zeros((VOX, w_ref.shape[2]), jnp.float32)
        for tap in range(TAPS):
            fwd += lax.dot_general(patch(ea, oa, tap), w_ref[b, tap], (((1,), (1,)), ((), ())),
                                   preferred_element_type=jnp.float32)
        hook()
        bwd = jnp.zeros((VOX, w_ref.shape[3]), jnp.float32)
        for tap in range(TAPS):
            bwd += jnp.dot(patch(eb, ob, TAPS - 1 - tap), w_ref[b, tap],
                           preferred_element_type=jnp.float32)
        return fwd, bwd

    def sec_copy(j):
        return pltpu.make_async_remote_copy(
            src_ref=upv.at[0, j], dst_ref=nxt.at[j], send_sem=sec_s.at[j], recv_sem=sec_r.at[j],
            device_id={"section": lax.rem(sec + nsec - 1, nsec)}, device_id_type=MESH)

    for tick in range(TICKS):
        if tick == 0:
            cur = first
        else:
            cur = nxt
            load_pool.wait()

            @pl.when(last)
            def _():
                nxt[...] = pool[plan[0, 0]]

            @pl.when(sec < nsec - 1)
            def _():
                for j in range(4):
                    sec_copy(j).wait_recv()
        y1 = cur[0].astype(jnp.float32)
        s1 = sigmoid(y1)
        a1 = y1 * s1
        dy2 = cur[3].astype(jnp.float32)
        share(2 * tick, a1.astype(jnp.bfloat16), dy2)
        fill(ea, oa, a1)
        fill(eb, ob, dy2)
        if tick == 0:
            loads[1].wait()
        fwd, bwd = convs(1, lambda: relay(2 * tick - 1) if tick else None)
        x2 = (cur[1].astype(jnp.float32) - fwd).astype(jnp.bfloat16)
        dx1 = (cur[2].astype(jnp.float32) + bwd * silu_grad(y1, s1)).astype(jnp.bfloat16)
        upv[tick, 1] = x2
        upv[tick, 2] = dx1
        if tick == 0:
            @pl.when(sec > 0)
            def _():
                sec_copy(1).start()
                sec_copy(2).start()
        u = x2.astype(jnp.float32)
        s2 = sigmoid(u)
        a2 = u * s2
        e1 = dx1.astype(jnp.float32)
        share(2 * tick + 1, a2.astype(jnp.bfloat16), e1)
        fill(ea, oa, a2)
        fill(eb, ob, e1)
        if tick == 0:
            loads[0].wait()
        fwd, bwd = convs(0, lambda: relay(2 * tick))
        u = upv[tick, 1].astype(jnp.float32)
        s2 = sigmoid(u)
        upv[tick, 0] = (cur[0].astype(jnp.float32) - fwd).astype(jnp.bfloat16)
        upv[tick, 3] = (cur[3].astype(jnp.float32) + bwd * silu_grad(u, s2)).astype(jnp.bfloat16)
        if tick == 0:
            @pl.when(sec > 0)
            def _():
                sec_copy(0).start()
                sec_copy(3).start()
        pltpu.make_async_copy(upv.at[tick], up.at[tick], up_sem.at[tick]).start()

    lane = lax.broadcasted_iota(jnp.int32, (block, VOX), 1)
    ld, lh, lw = lane // PLANE, (lane // TW) % TH, lane % TW

    def g_copy(b):
        return pltpu.make_async_remote_copy(
            src_ref=g_send.at[b], dst_ref=g_recv.at[b], send_sem=g_s.at[b], recv_sem=g_r.at[b],
            device_id={"dp": mate}, device_id_type=MESH)

    tiles = 3
    per = TAPS * block // tiles
    stages = 2 * TICKS
    relay(stages - 1)
    swap_errors(0)
    for stage in range(stages):
        b = stage % 2
        if stage + 1 < stages:
            swap_errors(stage + 1)
        d_to_mate(stage, 1 - core).wait_recv()
        arrive(stage)

        @pl.loop(0, n)
        def _(r):
            x = d_recv[stage, lax.rem(r, 2), r // (2 * nz), lax.rem(r // 2, nz)].astype(jnp.float32)
            cols = pl.ds(pl.multiple_of(r * VOX, VOX), VOX)
            for tap in range(TAPS):
                dd, dh, dw = tap_offset(tap)
                flat = dd * PLANE + dh * TW + dw
                s = x if flat == 0 else pltpu.roll(x, flat % VOX, 1)
                ok = None
                for c, by, size in ((ld, dd, TD), (lh, dh, TH), (lw, dw, TW)):
                    if by:
                        this = c >= 1 if by > 0 else c < size - 1
                        ok = this if ok is None else ok & this
                if ok is not None:
                    s = jnp.where(ok, s, 0.0)
                big[tap * block:(tap + 1) * block, cols] = s.astype(jnp.bfloat16)

        @pl.loop(0, tiles)
        def _(m):
            rows = pl.ds(pl.multiple_of(m * per, 16), per)
            got = jnp.dot(big[rows, :], a_recv[stage].reshape(n * VOX, LANES),
                          preferred_element_type=jnp.float32)
            if stage < 2:
                acc[b, rows, :] = got
            else:
                acc[b, rows, :] += got
        if stage >= 2 * TICKS - 2:
            view = acc.at[b]
            for tap in range(TAPS):
                lo = pl.multiple_of(tap * block + (1 - core) * half, 8)
                g_send[b, tap] = view[pl.ds(lo, half), :]
            g_copy(b).start()
    mine = pl.ds(pl.multiple_of(core * LANES, LANES), LANES)
    other = pl.ds(pl.multiple_of((1 - core) * LANES, LANES), LANES)
    for b in (0, 1):
        for tap in range(TAPS):
            lo = pl.multiple_of(tap * block + core * half, 8)
            grad[1 - b, tap, :, mine] = acc[b, pl.ds(lo, half), :]
    for b in (0, 1):
        g_copy(b).wait_recv()
        grad[1 - b, :, :, other] = g_recv[b]
    for b in (0, 1):
        g_copy(b).wait_send()
    for stage in range(stages):
        sent(stage)
    for tick in range(TICKS):
        pltpu.make_async_copy(upv.at[tick], up.at[tick], up_sem.at[tick]).wait()

    @pl.when(sec > 0)
    def _():
        for j in range(4):
            sec_copy(j).wait_send()


def body(incoming, feed, plan, weights, momentum):
    n = lax.axis_size("dp")
    nsec = lax.axis_size("section")
    channels = weights.shape[-1]
    block = 2 * channels // n
    ny = max(1, n // 8)
    nz = n // (2 * ny)
    stages = 2 * TICKS
    bf, f32 = jnp.bfloat16, jnp.float32
    vm = pl.BlockSpec(memory_space=pltpu.VMEM)
    hbm = pl.BlockSpec(memory_space=pl.ANY)
    dma = pltpu.SemaphoreType.DMA
    up, grad = pl.pallas_call(
        functools.partial(kernel, n, nsec),
        out_shape=(
            jax.ShapeDtypeStruct((TICKS, 4, VOX, channels), bf),
            jax.ShapeDtypeStruct((2, TAPS, block // 2, channels), f32),
        ),
        in_specs=[pl.BlockSpec(memory_space=pltpu.SMEM), hbm, hbm, hbm],
        out_specs=(hbm, vm),
        scratch_shapes=[
            pltpu.VMEM(weights.shape[1:], bf),
            pltpu.VMEM((4, VOX, channels), bf),
            pltpu.VMEM(feed.shape, bf),
            pltpu.VMEM((4, VOX, channels), bf),
            pltpu.VMEM((TICKS, 4, VOX, channels), bf),
            pltpu.VMEM((3, TD + 2, PLANE + 2 * TW, channels), bf),
            pltpu.VMEM((3, TD + 2, PLANE, channels), bf),
            pltpu.VMEM((3, TD + 2, PLANE + 2 * TW, channels), bf),
            pltpu.VMEM((3, TD + 2, PLANE, channels), bf),
            pltpu.VMEM((stages, 2, VOX, LANES), bf),
            pltpu.VMEM((stages, nz, ny, block, VOX), bf),
            pltpu.VMEM((stages, ny, nz, block, VOX), bf),
            pltpu.VMEM((stages, ny, nz, 2, VOX, LANES), bf),
            pltpu.VMEM((stages, 2, ny, nz, block, VOX), bf),
            pltpu.VMEM((TAPS * block, n * VOX), bf),
            pltpu.VMEM((2, TAPS * block, LANES), f32),
            pltpu.VMEM((2, TAPS, block // 2, LANES), f32),
            pltpu.VMEM((2, TAPS, block // 2, LANES), f32),
            dma((2,)), dma((2,)), dma((TICKS,)), dma((4,)), dma((4,)),
            dma((stages, 2 * (ny + nz))), dma((stages, ny, nz, 2)), dma((stages, ny, nz)), dma((stages, ny, nz)),
            dma((stages, nz)), dma((stages, nz)), dma((stages, ny)), dma((stages, ny)),
            dma((stages,)), dma((stages,)), dma((2,)), dma((2,)),
        ],
        compiler_params=pltpu.CompilerParams(
            collective_id=0, has_side_effects=True, vmem_limit_bytes=48 * 1024 * 1024),
        cost_estimate=pl.CostEstimate(flops=12 * TICKS * VOX * TAPS * channels * channels,
                                      bytes_accessed=weights.size * 2, transcendentals=0),
    )(plan, incoming, feed, weights)
    new_momentum = 0.9 * momentum[0] + grad / (n * TICKS)
    return (up[:, None], new_momentum[None])


def solution(mesh):
    in_specs = (
        P("section", None, "dp", None),
        P(None, None, "dp", None),
        P(None, "dp"),
        P("section", None, None, None, None),
        P("section", None, None, "dp", None),
    )
    out_specs = (P(None, "section", None, "dp", None), P("section", None, None, "dp", None))
    return jax.shard_map(body, mesh=mesh, in_specs=in_specs, out_specs=out_specs, check_vma=False)
```

```python
import functools

import jax
import jax.numpy as jnp
from jax import lax
from jax.experimental import pallas as pl
from jax.experimental.pallas import tpu as pltpu
from jax.sharding import PartitionSpec as P

TD = 2
TH = 8
TW = 8
TICKS = 2
VOX = TD * TH * TW
PLANE = TH * TW
TAPS = 27
LANES = 128
MESH = pl.DeviceIdType.MESH


def tap_offset(tap):
    return tap // 9 - 1, (tap // 3) % 3 - 1, tap % 3 - 1


def sigmoid(u):
    return 1.0 / (1.0 + jnp.exp(-u))


def silu_grad(u, s):
    return s * (1.0 + u * (1.0 - s))


def fill(even, odd, x):
    row = lax.broadcasted_iota(jnp.int32, x.shape, 0)
    w = row % TW
    edge = jnp.zeros((TW, x.shape[1]), jnp.float32)
    for wi, dw in enumerate((-1, 0, 1)):
        s = x
        if dw:
            s = pltpu.roll(x, (-dw) % VOX, 0)
            s = jnp.where((w + dw >= 0) & (w + dw < TW), s, 0.0)
        for d in range(TD):
            plane = s[d * PLANE:(d + 1) * PLANE]
            odd[wi, d + 1] = plane.astype(jnp.bfloat16)
            even[wi, d + 1] = jnp.concatenate([edge, plane, edge], 0).astype(jnp.bfloat16)


def patch(even, odd, tap):
    dd, dh, dw = tap_offset(tap)
    if dh == 0:
        cut = odd[dw + 1, dd + 1:dd + 1 + TD]
    else:
        lo = (dh + 1) * TW
        cut = even[dw + 1, dd + 1:dd + 1 + TD, lo:lo + PLANE]
    return cut.reshape(VOX, cut.shape[-1])


def kernel(n, nsec, plan, incoming, feed, weights, up, grad,
           w_ref, first, pool, nxt, upv, ea, oa, eb, ob, a_send, d_send, d_mid, a_recv, d_recv, big, acc,
           g_send, g_recv, w_sem, in_sem, up_sem, sec_s, sec_r, as_s, as_r, ar_s, ar_r,
           dz_s, dz_r, dy_s, dy_r, dm_s, dm_r, g_s, g_r):
    me = lax.axis_index("dp")
    sec = lax.axis_index("section")
    ny, nz = a_recv.shape[1:3]
    core = lax.rem(me, 2)
    y = lax.rem(me // 2, ny)
    z = me // (2 * ny)
    mate = me + 1 - 2 * core
    block = d_recv.shape[-2]
    half = block // 2
    last = sec == nsec - 1

    def at(zz, yy, cc):
        return (zz * ny + yy) * 2 + cc

    def z_of(k):
        return lax.rem(z + k, nz)

    def y_of(k):
        return lax.rem(y + k, ny)

    load_in = pltpu.make_async_copy(incoming.at[0], first, in_sem.at[0])
    load_pool = pltpu.make_async_copy(feed, pool, in_sem.at[1])
    loads = [pltpu.make_async_copy(weights.at[0, b], w_ref.at[b], w_sem.at[b]) for b in (0, 1)]
    load_in.start()
    loads[1].start()
    loads[0].start()
    load_pool.start()

    barrier = pltpu.get_barrier_semaphore()
    peers = [mate]
    peers += [at(z_of(k), y, cc) for k in range(1, nz) for cc in (0, 1)]
    peers += [at(z, y_of(k), cc) for k in range(1, ny) for cc in (0, 1)]
    for peer in peers:
        pl.semaphore_signal(barrier, inc=1, device_id={"dp": peer}, device_id_type=MESH)

    @pl.when(sec > 0)
    def _():
        pl.semaphore_signal(barrier, inc=1, device_id={"section": sec - 1}, device_id_type=MESH)

    @pl.when(sec < nsec - 1)
    def _():
        pl.semaphore_signal(barrier, inc=1, device_id={"section": sec + 1}, device_id_type=MESH)

    for wi in range(3):
        for ref in (ea, oa, eb, ob):
            for d in (0, TD + 1):
                ref[wi, d] = jnp.zeros(ref.shape[2:], jnp.bfloat16)
    load_in.wait()
    extra = jnp.where(sec > 0, 1, 0) + jnp.where(sec < nsec - 1, 1, 0)
    pl.semaphore_wait(barrier, len(peers) + extra)

    def a_direct(stage, idx, peer, to, slot):
        return pltpu.make_async_remote_copy(
            src_ref=a_send.at[stage, to], dst_ref=a_recv.at[(stage,) + slot],
            send_sem=as_s.at[stage, idx], recv_sem=as_r.at[(stage,) + slot],
            device_id={"dp": peer}, device_id_type=MESH)

    def a_relay(stage, yy, slot):
        return pltpu.make_async_remote_copy(
            src_ref=a_recv.at[(stage,) + slot], dst_ref=a_recv.at[(stage,) + slot],
            send_sem=ar_s.at[stage, yy, slot[1]], recv_sem=ar_r.at[(stage,) + slot],
            device_id={"dp": at(z, yy, core)}, device_id_type=MESH)

    def d_along_z(stage, zz, slot):
        return pltpu.make_async_remote_copy(
            src_ref=d_send.at[stage, zz], dst_ref=d_mid.at[stage, :, slot],
            send_sem=dz_s.at[stage, zz], recv_sem=dz_r.at[stage, slot],
            device_id={"dp": at(zz, y, core)}, device_id_type=MESH)

    def d_along_y(stage, yy, slot):
        return pltpu.make_async_remote_copy(
            src_ref=d_mid.at[stage, yy], dst_ref=d_recv.at[stage, core, slot],
            send_sem=dy_s.at[stage, yy], recv_sem=dy_r.at[stage, slot],
            device_id={"dp": at(z, yy, core)}, device_id_type=MESH)

    def d_to_mate(stage, whose):
        return pltpu.make_async_remote_copy(
            src_ref=d_recv.at[stage, whose], dst_ref=d_recv.at[stage, whose],
            send_sem=dm_s.at[stage], recv_sem=dm_r.at[stage],
            device_id={"dp": mate}, device_id_type=MESH)

    def directs(stage):
        mine = (y, z, core)
        out = []
        for k in range(1, nz):
            for cc in (0, 1):
                out.append(a_direct(stage, len(out), at(z_of(k), y, cc), cc, mine))
        for k in range(1, ny):
            for cc in (0, 1):
                out.append(a_direct(stage, len(out), at(z, y_of(k), cc), cc, mine))
        out.append(a_direct(stage, len(out), mate, 1 - core, mine))
        return out

    def share(stage, act, err):
        a_send[stage, 0] = act[:, :LANES]
        a_send[stage, 1] = act[:, LANES:]
        turned = jnp.transpose(err).astype(jnp.bfloat16)
        d_send[stage] = turned.reshape(d_send.shape[1:])
        for k in range(1, nz):
            d_along_z(stage, z_of(k), z).start()
        for copy in directs(stage):
            copy.start()
        a_recv[stage, y, z, core] = a_send[stage, core]
        for yy in range(ny):
            d_mid[stage, yy, z] = d_send[stage, z, yy]

    def relay(stage):
        for k in range(1, nz):
            d_along_z(stage, z, z_of(k)).wait_recv()
        for k in range(1, ny):
            d_along_y(stage, y_of(k), y).start()
        d_recv[stage, core, y] = d_mid[stage, y]
        for k in range(1, nz):
            for cc in (0, 1):
                a_direct(stage, 0, mate, 0, (y, z_of(k), cc)).wait_recv()
            for j in range(1, ny):
                a_relay(stage, y_of(j), (y, z_of(k))).start()

    def swap_errors(stage):
        for k in range(1, ny):
            d_along_y(stage, y, y_of(k)).wait_recv()
        d_to_mate(stage, core).start()

    def arrive(stage):
        a_direct(stage, 0, mate, 0, (y, z, 1 - core)).wait_recv()
        for j in range(1, ny):
            for cc in (0, 1):
                a_direct(stage, 0, mate, 0, (y_of(j), z, cc)).wait_recv()
            for k in range(1, nz):
                a_relay(stage, y, (y_of(j), z_of(k))).wait_recv()

    def sent(stage):
        for k in range(1, nz):
            d_along_z(stage, z_of(k), z).wait_send()
        for copy in directs(stage):
            copy.wait_send()
        for j in range(1, ny):
            d_along_y(stage, y_of(j), y).wait_send()
            for k in range(1, nz):
                a_relay(stage, y_of(j), (y, z_of(k))).wait_send()
        d_to_mate(stage, core).wait_send()

    def convs(b, hook):
        fwd = jnp.zeros((VOX, w_ref.shape[2]), jnp.float32)
        for tap in range(TAPS):
            fwd += lax.dot_general(patch(ea, oa, tap), w_ref[b, tap], (((1,), (1,)), ((), ())),
                                   preferred_element_type=jnp.float32)
        hook()
        bwd = jnp.zeros((VOX, w_ref.shape[3]), jnp.float32)
        for tap in range(TAPS):
            bwd += jnp.dot(patch(eb, ob, TAPS - 1 - tap), w_ref[b, tap],
                           preferred_element_type=jnp.float32)
        return fwd, bwd

    def sec_copy(j):
        return pltpu.make_async_remote_copy(
            src_ref=upv.at[0, j], dst_ref=nxt.at[j], send_sem=sec_s.at[j], recv_sem=sec_r.at[j],
            device_id={"section": lax.rem(sec + nsec - 1, nsec)}, device_id_type=MESH)

    for tick in range(TICKS):
        if tick == 0:
            cur = first
        else:
            cur = nxt
            load_pool.wait()

            @pl.when(last)
            def _():
                nxt[...] = pool[plan[0, 0]]

            @pl.when(sec < nsec - 1)
            def _():
                for j in range(4):
                    sec_copy(j).wait_recv()
        y1 = cur[0].astype(jnp.float32)
        s1 = sigmoid(y1)
        a1 = y1 * s1
        dy2 = cur[3].astype(jnp.float32)
        share(2 * tick, a1.astype(jnp.bfloat16), dy2)
        fill(ea, oa, a1)
        fill(eb, ob, dy2)
        if tick == 0:
            loads[1].wait()
        fwd, bwd = convs(1, lambda: relay(2 * tick - 1) if tick else None)
        x2 = (cur[1].astype(jnp.float32) - fwd).astype(jnp.bfloat16)
        dx1 = (cur[2].astype(jnp.float32) + bwd * silu_grad(y1, s1)).astype(jnp.bfloat16)
        upv[tick, 1] = x2
        upv[tick, 2] = dx1
        if tick == 0:
            @pl.when(sec > 0)
            def _():
                sec_copy(1).start()
                sec_copy(2).start()
        u = x2.astype(jnp.float32)
        s2 = sigmoid(u)
        a2 = u * s2
        e1 = dx1.astype(jnp.float32)
        share(2 * tick + 1, a2.astype(jnp.bfloat16), e1)
        fill(ea, oa, a2)
        fill(eb, ob, e1)
        if tick == 0:
            loads[0].wait()
        fwd, bwd = convs(0, lambda: relay(2 * tick))
        u = upv[tick, 1].astype(jnp.float32)
        s2 = sigmoid(u)
        upv[tick, 0] = (cur[0].astype(jnp.float32) - fwd).astype(jnp.bfloat16)
        upv[tick, 3] = (cur[3].astype(jnp.float32) + bwd * silu_grad(u, s2)).astype(jnp.bfloat16)
        if tick == 0:
            @pl.when(sec > 0)
            def _():
                sec_copy(0).start()
                sec_copy(3).start()
        pltpu.make_async_copy(upv.at[tick], up.at[tick], up_sem.at[tick]).start()

    lane = lax.broadcasted_iota(jnp.int32, (8, VOX), 1)
    masks = {}
    for step, size in ((1, TW), (TW, TH), (PLANE, TD)):
        at_axis = (lane // step) % size
        masks[step] = at_axis >= 1
        masks[-step] = at_axis < size - 1

    def moved(x, by):
        if by == 0:
            return x
        return jnp.where(masks[by], pltpu.roll(x, by % VOX, 2), 0.0)

    def g_copy(b):
        return pltpu.make_async_remote_copy(
            src_ref=g_send.at[b], dst_ref=g_recv.at[b], send_sem=g_s.at[b], recv_sem=g_r.at[b],
            device_id={"dp": mate}, device_id_type=MESH)

    tiles = 3
    per = TAPS * block // tiles
    stages = 2 * TICKS
    relay(stages - 1)
    swap_errors(0)
    for stage in range(stages):
        b = stage % 2
        if stage + 1 < stages:
            swap_errors(stage + 1)
        d_to_mate(stage, 1 - core).wait_recv()
        arrive(stage)

        @pl.loop(0, n // 2)
        def _(r):
            yy, zz = r // nz, lax.rem(r, nz)
            for cc in (0, 1):
                x = d_recv[stage, cc, yy, zz].astype(jnp.float32).reshape(block // 8, 8, VOX)
                cols = pl.ds(pl.multiple_of((2 * r + cc) * VOX, VOX), VOX)
                for dw in (-1, 0, 1):
                    xw = moved(x, dw)
                    for dh in (-1, 0, 1):
                        xh = moved(xw, dh * TW)
                        for dd in (-1, 0, 1):
                            lo = (9 * (dd + 1) + 3 * (dh + 1) + dw + 1) * block
                            s = moved(xh, dd * PLANE).reshape(block, VOX)
                            big[lo:lo + block, cols] = s.astype(jnp.bfloat16)

        @pl.loop(0, tiles)
        def _(m):
            rows = pl.ds(pl.multiple_of(m * per, 16), per)
            got = jnp.dot(big[rows, :], a_recv[stage].reshape(n * VOX, LANES),
                          preferred_element_type=jnp.float32)
            if stage < 2:
                acc[b, rows, :] = got
            else:
                acc[b, rows, :] += got
        if stage >= 2 * TICKS - 2:
            view = acc.at[b]
            for tap in range(TAPS):
                lo = pl.multiple_of(tap * block + (1 - core) * half, 8)
                g_send[b, tap] = view[pl.ds(lo, half), :]
            g_copy(b).start()
    mine = pl.ds(pl.multiple_of(core * LANES, LANES), LANES)
    other = pl.ds(pl.multiple_of((1 - core) * LANES, LANES), LANES)
    for b in (0, 1):
        for tap in range(TAPS):
            lo = pl.multiple_of(tap * block + core * half, 8)
            grad[1 - b, tap, :, mine] = acc[b, pl.ds(lo, half), :]
    for b in (0, 1):
        g_copy(b).wait_recv()
        grad[1 - b, :, :, other] = g_recv[b]
    for b in (0, 1):
        g_copy(b).wait_send()
    for stage in range(stages):
        sent(stage)
    for tick in range(TICKS):
        pltpu.make_async_copy(upv.at[tick], up.at[tick], up_sem.at[tick]).wait()

    @pl.when(sec > 0)
    def _():
        for j in range(4):
            sec_copy(j).wait_send()


def body(incoming, feed, plan, weights, momentum):
    n = lax.axis_size("dp")
    nsec = lax.axis_size("section")
    channels = weights.shape[-1]
    block = 2 * channels // n
    ny = max(1, n // 8)
    nz = n // (2 * ny)
    stages = 2 * TICKS
    bf, f32 = jnp.bfloat16, jnp.float32
    vm = pl.BlockSpec(memory_space=pltpu.VMEM)
    hbm = pl.BlockSpec(memory_space=pl.ANY)
    dma = pltpu.SemaphoreType.DMA
    up, grad = pl.pallas_call(
        functools.partial(kernel, n, nsec),
        out_shape=(
            jax.ShapeDtypeStruct((TICKS, 4, VOX, channels), bf),
            jax.ShapeDtypeStruct((2, TAPS, block // 2, channels), f32),
        ),
        in_specs=[pl.BlockSpec(memory_space=pltpu.SMEM)] + [pl.BlockSpec(memory_space=pltpu.HBM)] * 3,
        out_specs=(hbm, vm),
        scratch_shapes=[
            pltpu.VMEM(weights.shape[1:], bf),
            pltpu.VMEM((4, VOX, channels), bf),
            pltpu.VMEM(feed.shape, bf),
            pltpu.VMEM((4, VOX, channels), bf),
            pltpu.VMEM((TICKS, 4, VOX, channels), bf),
            pltpu.VMEM((3, TD + 2, PLANE + 2 * TW, channels), bf),
            pltpu.VMEM((3, TD + 2, PLANE, channels), bf),
            pltpu.VMEM((3, TD + 2, PLANE + 2 * TW, channels), bf),
            pltpu.VMEM((3, TD + 2, PLANE, channels), bf),
            pltpu.VMEM((stages, 2, VOX, LANES), bf),
            pltpu.VMEM((stages, nz, ny, block, VOX), bf),
            pltpu.VMEM((stages, ny, nz, block, VOX), bf),
            pltpu.VMEM((stages, ny, nz, 2, VOX, LANES), bf),
            pltpu.VMEM((stages, 2, ny, nz, block, VOX), bf),
            pltpu.VMEM((TAPS * block, n * VOX), bf),
            pltpu.VMEM((2, TAPS * block, LANES), f32),
            pltpu.VMEM((2, TAPS, block // 2, LANES), f32),
            pltpu.VMEM((2, TAPS, block // 2, LANES), f32),
            dma((2,)), dma((2,)), dma((TICKS,)), dma((4,)), dma((4,)),
            dma((stages, 2 * (ny + nz))), dma((stages, ny, nz, 2)), dma((stages, ny, nz)), dma((stages, ny, nz)),
            dma((stages, nz)), dma((stages, nz)), dma((stages, ny)), dma((stages, ny)),
            dma((stages,)), dma((stages,)), dma((2,)), dma((2,)),
        ],
        compiler_params=pltpu.CompilerParams(
            collective_id=0, has_side_effects=True, vmem_limit_bytes=63 * 1024 * 1024),
        cost_estimate=pl.CostEstimate(flops=12 * TICKS * VOX * TAPS * channels * channels,
                                      bytes_accessed=weights.size * 2, transcendentals=0),
    )(plan, incoming, feed, weights)
    new_momentum = 0.9 * momentum[0] + grad / (n * TICKS)
    return (up[:, None], new_momentum[None])


def solution(mesh):
    in_specs = (
        P("section", None, "dp", None),
        P(None, None, "dp", None),
        P(None, "dp"),
        P("section", None, None, None, None),
        P("section", None, None, "dp", None),
    )
    out_specs = (P(None, "section", None, "dp", None), P("section", None, None, "dp", None))
    return jax.shard_map(body, mesh=mesh, in_specs=in_specs, out_specs=out_specs, check_vma=False)
```

```python
import functools

import jax
import jax.numpy as jnp
from jax import lax
from jax.experimental import pallas as pl
from jax.experimental.pallas import tpu as pltpu
from jax.sharding import PartitionSpec as P

TD = 2
TH = 8
TW = 8
TICKS = 2
VOX = TD * TH * TW
PLANE = TH * TW
TAPS = 27
LANES = 128
MESH = pl.DeviceIdType.MESH


def tap_offset(tap):
    return tap // 9 - 1, (tap // 3) % 3 - 1, tap % 3 - 1


def sigmoid(u):
    return 1.0 / (1.0 + jnp.exp(-u))


def silu_grad(u, s):
    return s * (1.0 + u * (1.0 - s))


def fill(even, odd, x):
    row = lax.broadcasted_iota(jnp.int32, x.shape, 0)
    w = row % TW
    edge = jnp.zeros((TW, x.shape[1]), jnp.float32)
    for wi, dw in enumerate((-1, 0, 1)):
        s = x
        if dw:
            s = pltpu.roll(x, (-dw) % VOX, 0)
            s = jnp.where((w + dw >= 0) & (w + dw < TW), s, 0.0)
        for d in range(TD):
            plane = s[d * PLANE:(d + 1) * PLANE]
            odd[wi, d + 1] = plane.astype(jnp.bfloat16)
            even[wi, d + 1] = jnp.concatenate([edge, plane, edge], 0).astype(jnp.bfloat16)


def patch(even, odd, tap):
    dd, dh, dw = tap_offset(tap)
    if dh == 0:
        cut = odd[dw + 1, dd + 1:dd + 1 + TD]
    else:
        lo = (dh + 1) * TW
        cut = even[dw + 1, dd + 1:dd + 1 + TD, lo:lo + PLANE]
    return cut.reshape(VOX, cut.shape[-1])


def kernel(n, nsec, plan, incoming, feed, weights, up, grad,
           w_ref, w_cat, cols, first, pool, nxt, upv, ea, oa, eb, ob, a_send, d_send, d_mid, a_recv, d_recv, big, acc,
           g_send, g_recv, w_sem, wc_sem, in_sem, up_sem, sec_s, sec_r, as_s, as_r, ar_s, ar_r,
           dz_s, dz_r, dy_s, dy_r, dm_s, dm_r, g_s, g_r):
    me = lax.axis_index("dp")
    sec = lax.axis_index("section")
    ny, nz = a_recv.shape[1:3]
    core = lax.rem(me, 2)
    y = lax.rem(me // 2, ny)
    z = me // (2 * ny)
    mate = me + 1 - 2 * core
    block = d_recv.shape[-2]
    half = block // 2
    last = sec == nsec - 1

    def at(zz, yy, cc):
        return (zz * ny + yy) * 2 + cc

    def z_of(k):
        return lax.rem(z + k, nz)

    def y_of(k):
        return lax.rem(y + k, ny)

    load_in = pltpu.make_async_copy(incoming.at[0], first, in_sem.at[0])
    load_pool = pltpu.make_async_copy(feed, pool, in_sem.at[1])
    loads = [pltpu.make_async_copy(weights.at[0, b], w_ref.at[b], w_sem.at[b]) for b in (0, 1)]
    load_in.start()
    channels = w_ref.shape[-1]

    def load_cat(b):
        for tap in range(TAPS):
            pltpu.make_async_copy(weights.at[0, b, tap], w_cat.at[b, :, tap * channels:(tap + 1) * channels],
                                  wc_sem.at[b]).start()

    load_cat(1)
    loads[1].start()
    load_cat(0)
    loads[0].start()
    load_pool.start()

    barrier = pltpu.get_barrier_semaphore()
    peers = [mate]
    peers += [at(z_of(k), y, cc) for k in range(1, nz) for cc in (0, 1)]
    peers += [at(z, y_of(k), cc) for k in range(1, ny) for cc in (0, 1)]
    for peer in peers:
        pl.semaphore_signal(barrier, inc=1, device_id={"dp": peer}, device_id_type=MESH)

    @pl.when(sec > 0)
    def _():
        pl.semaphore_signal(barrier, inc=1, device_id={"section": sec - 1}, device_id_type=MESH)

    @pl.when(sec < nsec - 1)
    def _():
        pl.semaphore_signal(barrier, inc=1, device_id={"section": sec + 1}, device_id_type=MESH)

    for wi in range(3):
        for ref in (ea, oa, eb, ob):
            for d in (0, TD + 1):
                ref[wi, d] = jnp.zeros(ref.shape[2:], jnp.bfloat16)
    load_in.wait()
    extra = jnp.where(sec > 0, 1, 0) + jnp.where(sec < nsec - 1, 1, 0)
    pl.semaphore_wait(barrier, len(peers) + extra)

    def a_direct(stage, idx, peer, to, slot):
        return pltpu.make_async_remote_copy(
            src_ref=a_send.at[stage, to], dst_ref=a_recv.at[(stage,) + slot],
            send_sem=as_s.at[stage, idx], recv_sem=as_r.at[(stage,) + slot],
            device_id={"dp": peer}, device_id_type=MESH)

    def a_relay(stage, yy, slot):
        return pltpu.make_async_remote_copy(
            src_ref=a_recv.at[(stage,) + slot], dst_ref=a_recv.at[(stage,) + slot],
            send_sem=ar_s.at[stage, yy, slot[1]], recv_sem=ar_r.at[(stage,) + slot],
            device_id={"dp": at(z, yy, core)}, device_id_type=MESH)

    def d_along_z(stage, zz, slot):
        return pltpu.make_async_remote_copy(
            src_ref=d_send.at[stage, zz], dst_ref=d_mid.at[stage, :, slot],
            send_sem=dz_s.at[stage, zz], recv_sem=dz_r.at[stage, slot],
            device_id={"dp": at(zz, y, core)}, device_id_type=MESH)

    def d_along_y(stage, yy, slot):
        return pltpu.make_async_remote_copy(
            src_ref=d_mid.at[stage, yy], dst_ref=d_recv.at[stage, core, slot],
            send_sem=dy_s.at[stage, yy], recv_sem=dy_r.at[stage, slot],
            device_id={"dp": at(z, yy, core)}, device_id_type=MESH)

    def d_to_mate(stage, whose):
        return pltpu.make_async_remote_copy(
            src_ref=d_recv.at[stage, whose], dst_ref=d_recv.at[stage, whose],
            send_sem=dm_s.at[stage], recv_sem=dm_r.at[stage],
            device_id={"dp": mate}, device_id_type=MESH)

    def directs(stage):
        mine = (y, z, core)
        out = []
        for k in range(1, nz):
            for cc in (0, 1):
                out.append(a_direct(stage, len(out), at(z_of(k), y, cc), cc, mine))
        for k in range(1, ny):
            for cc in (0, 1):
                out.append(a_direct(stage, len(out), at(z, y_of(k), cc), cc, mine))
        out.append(a_direct(stage, len(out), mate, 1 - core, mine))
        return out

    def share(stage, act, err):
        a_send[stage, 0] = act[:, :LANES]
        a_send[stage, 1] = act[:, LANES:]
        turned = jnp.transpose(err).astype(jnp.bfloat16)
        d_send[stage] = turned.reshape(d_send.shape[1:])
        for k in range(1, nz):
            d_along_z(stage, z_of(k), z).start()
        for copy in directs(stage):
            copy.start()
        a_recv[stage, y, z, core] = a_send[stage, core]
        for yy in range(ny):
            d_mid[stage, yy, z] = d_send[stage, z, yy]

    def relay(stage):
        for k in range(1, nz):
            d_along_z(stage, z, z_of(k)).wait_recv()
        for k in range(1, ny):
            d_along_y(stage, y_of(k), y).start()
        d_recv[stage, core, y] = d_mid[stage, y]
        for k in range(1, nz):
            for cc in (0, 1):
                a_direct(stage, 0, mate, 0, (y, z_of(k), cc)).wait_recv()
            for j in range(1, ny):
                a_relay(stage, y_of(j), (y, z_of(k))).start()

    def swap_errors(stage):
        for k in range(1, ny):
            d_along_y(stage, y, y_of(k)).wait_recv()
        d_to_mate(stage, core).start()

    def arrive(stage):
        a_direct(stage, 0, mate, 0, (y, z, 1 - core)).wait_recv()
        for j in range(1, ny):
            for cc in (0, 1):
                a_direct(stage, 0, mate, 0, (y_of(j), z, cc)).wait_recv()
            for k in range(1, nz):
                a_relay(stage, y, (y_of(j), z_of(k))).wait_recv()

    def sent(stage):
        for k in range(1, nz):
            d_along_z(stage, z_of(k), z).wait_send()
        for copy in directs(stage):
            copy.wait_send()
        for j in range(1, ny):
            d_along_y(stage, y_of(j), y).wait_send()
            for k in range(1, nz):
                a_relay(stage, y_of(j), (y, z_of(k))).wait_send()
        d_to_mate(stage, core).wait_send()

    def gather(even, odd, flip):
        for tap in range(TAPS):
            lo = tap * channels
            cols[:, lo:lo + channels] = patch(even, odd, TAPS - 1 - tap if flip else tap)

    def convs(b, hook):
        gather(ea, oa, False)
        fwd = lax.dot_general(cols[...], w_cat[b], (((1,), (1,)), ((), ())),
                              preferred_element_type=jnp.float32)
        hook()
        gather(eb, ob, True)
        bwd = jnp.dot(cols[...], w_ref[b].reshape(TAPS * channels, channels),
                      preferred_element_type=jnp.float32)
        return fwd, bwd

    def sec_copy(j):
        return pltpu.make_async_remote_copy(
            src_ref=upv.at[0, j], dst_ref=nxt.at[j], send_sem=sec_s.at[j], recv_sem=sec_r.at[j],
            device_id={"section": lax.rem(sec + nsec - 1, nsec)}, device_id_type=MESH)

    for tick in range(TICKS):
        if tick == 0:
            cur = first
        else:
            cur = nxt
            load_pool.wait()

            @pl.when(last)
            def _():
                nxt[...] = pool[plan[0, 0]]

            @pl.when(sec < nsec - 1)
            def _():
                for j in range(4):
                    sec_copy(j).wait_recv()
        y1 = cur[0].astype(jnp.float32)
        s1 = sigmoid(y1)
        a1 = y1 * s1
        dy2 = cur[3].astype(jnp.float32)
        share(2 * tick, a1.astype(jnp.bfloat16), dy2)
        fill(ea, oa, a1)
        fill(eb, ob, dy2)
        if tick == 0:
            loads[1].wait()
            pltpu.make_async_copy(w_cat.at[1], w_cat.at[1], wc_sem.at[1]).wait()
        fwd, bwd = convs(1, lambda: relay(2 * tick - 1) if tick else None)
        x2 = (cur[1].astype(jnp.float32) - fwd).astype(jnp.bfloat16)
        dx1 = (cur[2].astype(jnp.float32) + bwd * silu_grad(y1, s1)).astype(jnp.bfloat16)
        upv[tick, 1] = x2
        upv[tick, 2] = dx1
        if tick == 0:
            @pl.when(sec > 0)
            def _():
                sec_copy(1).start()
                sec_copy(2).start()
        u = x2.astype(jnp.float32)
        s2 = sigmoid(u)
        a2 = u * s2
        e1 = dx1.astype(jnp.float32)
        share(2 * tick + 1, a2.astype(jnp.bfloat16), e1)
        fill(ea, oa, a2)
        fill(eb, ob, e1)
        if tick == 0:
            loads[0].wait()
            pltpu.make_async_copy(w_cat.at[0], w_cat.at[0], wc_sem.at[0]).wait()
        fwd, bwd = convs(0, lambda: relay(2 * tick))
        u = upv[tick, 1].astype(jnp.float32)
        s2 = sigmoid(u)
        upv[tick, 0] = (cur[0].astype(jnp.float32) - fwd).astype(jnp.bfloat16)
        upv[tick, 3] = (cur[3].astype(jnp.float32) + bwd * silu_grad(u, s2)).astype(jnp.bfloat16)
        if tick == 0:
            @pl.when(sec > 0)
            def _():
                sec_copy(0).start()
                sec_copy(3).start()
        pltpu.make_async_copy(upv.at[tick], up.at[tick], up_sem.at[tick]).start()

    lane = lax.broadcasted_iota(jnp.int32, (8, VOX), 1)
    masks = {}
    for step, size in ((1, TW), (TW, TH), (PLANE, TD)):
        at_axis = (lane // step) % size
        masks[step] = at_axis >= 1
        masks[-step] = at_axis < size - 1

    def moved(x, by):
        if by == 0:
            return x
        return jnp.where(masks[by], pltpu.roll(x, by % VOX, 2), 0.0)

    def g_copy(b):
        return pltpu.make_async_remote_copy(
            src_ref=g_send.at[b], dst_ref=g_recv.at[b], send_sem=g_s.at[b], recv_sem=g_r.at[b],
            device_id={"dp": mate}, device_id_type=MESH)

    tiles = 3
    per = TAPS * block // tiles
    stages = 2 * TICKS
    relay(stages - 1)
    swap_errors(0)
    for stage in range(stages):
        b = stage % 2
        if stage + 1 < stages:
            swap_errors(stage + 1)
        d_to_mate(stage, 1 - core).wait_recv()
        arrive(stage)

        @pl.loop(0, n // 2)
        def _(r):
            yy, zz = r // nz, lax.rem(r, nz)
            for cc in (0, 1):
                x = d_recv[stage, cc, yy, zz].astype(jnp.float32).reshape(block // 8, 8, VOX)
                cols = pl.ds(pl.multiple_of((2 * r + cc) * VOX, VOX), VOX)
                for dw in (-1, 0, 1):
                    xw = moved(x, dw)
                    for dh in (-1, 0, 1):
                        xh = moved(xw, dh * TW)
                        for dd in (-1, 0, 1):
                            lo = (9 * (dd + 1) + 3 * (dh + 1) + dw + 1) * block
                            s = moved(xh, dd * PLANE).reshape(block, VOX)
                            big[lo:lo + block, cols] = s.astype(jnp.bfloat16)

        @pl.loop(0, tiles)
        def _(m):
            rows = pl.ds(pl.multiple_of(m * per, 16), per)
            got = jnp.dot(big[rows, :], a_recv[stage].reshape(n * VOX, LANES),
                          preferred_element_type=jnp.float32)
            if stage < 2:
                acc[b, rows, :] = got
            else:
                acc[b, rows, :] += got
        if stage >= 2 * TICKS - 2:
            view = acc.at[b]
            for tap in range(TAPS):
                lo = pl.multiple_of(tap * block + (1 - core) * half, 8)
                g_send[b, tap] = view[pl.ds(lo, half), :]
            g_copy(b).start()
    mine = pl.ds(pl.multiple_of(core * LANES, LANES), LANES)
    other = pl.ds(pl.multiple_of((1 - core) * LANES, LANES), LANES)
    for b in (0, 1):
        for tap in range(TAPS):
            lo = pl.multiple_of(tap * block + core * half, 8)
            grad[1 - b, tap, :, mine] = acc[b, pl.ds(lo, half), :]
    for b in (0, 1):
        g_copy(b).wait_recv()
        grad[1 - b, :, :, other] = g_recv[b]
    for b in (0, 1):
        g_copy(b).wait_send()
    for stage in range(stages):
        sent(stage)
    for tick in range(TICKS):
        pltpu.make_async_copy(upv.at[tick], up.at[tick], up_sem.at[tick]).wait()

    @pl.when(sec > 0)
    def _():
        for j in range(4):
            sec_copy(j).wait_send()


def body(incoming, feed, plan, weights, momentum):
    n = lax.axis_size("dp")
    nsec = lax.axis_size("section")
    channels = weights.shape[-1]
    block = 2 * channels // n
    ny = max(1, n // 8)
    nz = n // (2 * ny)
    stages = 2 * TICKS
    bf, f32 = jnp.bfloat16, jnp.float32
    vm = pl.BlockSpec(memory_space=pltpu.VMEM)
    hbm = pl.BlockSpec(memory_space=pl.ANY)
    dma = pltpu.SemaphoreType.DMA
    incoming = pltpu.with_memory_space_constraint(incoming, pltpu.HBM)
    feed = pltpu.with_memory_space_constraint(feed, pltpu.HBM)
    up, grad = pl.pallas_call(
        functools.partial(kernel, n, nsec),
        out_shape=(
            jax.ShapeDtypeStruct((TICKS, 4, VOX, channels), bf),
            jax.ShapeDtypeStruct((2, TAPS, block // 2, channels), f32),
        ),
        in_specs=[pl.BlockSpec(memory_space=pltpu.SMEM)] + [pl.BlockSpec(memory_space=pltpu.HBM)] * 3,
        out_specs=(hbm, vm),
        scratch_shapes=[
            pltpu.VMEM(weights.shape[1:], bf),
            pltpu.VMEM((2, channels, TAPS * channels), bf),
            pltpu.VMEM((VOX, TAPS * channels), bf),
            pltpu.VMEM((4, VOX, channels), bf),
            pltpu.VMEM(feed.shape, bf),
            pltpu.VMEM((4, VOX, channels), bf),
            pltpu.VMEM((TICKS, 4, VOX, channels), bf),
            pltpu.VMEM((3, TD + 2, PLANE + 2 * TW, channels), bf),
            pltpu.VMEM((3, TD + 2, PLANE, channels), bf),
            pltpu.VMEM((3, TD + 2, PLANE + 2 * TW, channels), bf),
            pltpu.VMEM((3, TD + 2, PLANE, channels), bf),
            pltpu.VMEM((stages, 2, VOX, LANES), bf),
            pltpu.VMEM((stages, nz, ny, block, VOX), bf),
            pltpu.VMEM((stages, ny, nz, block, VOX), bf),
            pltpu.VMEM((stages, ny, nz, 2, VOX, LANES), bf),
            pltpu.VMEM((stages, 2, ny, nz, block, VOX), bf),
            pltpu.VMEM((TAPS * block, n * VOX), bf),
            pltpu.VMEM((2, TAPS * block, LANES), f32),
            pltpu.VMEM((2, TAPS, block // 2, LANES), f32),
            pltpu.VMEM((2, TAPS, block // 2, LANES), f32),
            dma((2,)), dma((2,)), dma((2,)), dma((TICKS,)), dma((4,)), dma((4,)),
            dma((stages, 2 * (ny + nz))), dma((stages, ny, nz, 2)), dma((stages, ny, nz)), dma((stages, ny, nz)),
            dma((stages, nz)), dma((stages, nz)), dma((stages, ny)), dma((stages, ny)),
            dma((stages,)), dma((stages,)), dma((2,)), dma((2,)),
        ],
        compiler_params=pltpu.CompilerParams(
            collective_id=0, has_side_effects=True, vmem_limit_bytes=48 * 1024 * 1024),
        cost_estimate=pl.CostEstimate(flops=12 * TICKS * VOX * TAPS * channels * channels,
                                      bytes_accessed=weights.size * 2, transcendentals=0),
    )(plan, incoming, feed, weights)
    new_momentum = 0.9 * momentum[0] + grad / (n * TICKS)
    return (up[:, None], new_momentum[None])


def solution(mesh):
    in_specs = (
        P("section", None, "dp", None),
        P(None, None, "dp", None),
        P(None, "dp"),
        P("section", None, None, None, None),
        P("section", None, None, "dp", None),
    )
    out_specs = (P(None, "section", None, "dp", None), P("section", None, None, "dp", None))
    return jax.shard_map(body, mesh=mesh, in_specs=in_specs, out_specs=out_specs, check_vma=False)
```

```python
import functools

import jax
import jax.numpy as jnp
from jax import lax
from jax.experimental import pallas as pl
from jax.experimental.pallas import tpu as pltpu
from jax.sharding import PartitionSpec as P

TD = 2
TH = 8
TW = 8
TICKS = 2
VOX = TD * TH * TW
PLANE = TH * TW
TAPS = 27
LANES = 128
MESH = pl.DeviceIdType.MESH


def sigmoid(u):
    return 1.0 / (1.0 + jnp.exp(-u))


def silu_grad(u, s):
    return s * (1.0 + u * (1.0 - s))


def fill(even, odd, x):
    row = lax.broadcasted_iota(jnp.int32, x.shape, 0)
    w = row % TW
    edge = jnp.zeros((TW, x.shape[1]), jnp.float32)
    for wi, dw in enumerate((-1, 0, 1)):
        s = x
        if dw:
            s = pltpu.roll(x, (-dw) % VOX, 0)
            s = jnp.where((w + dw >= 0) & (w + dw < TW), s, 0.0)
        for d in range(TD):
            plane = s[d * PLANE:(d + 1) * PLANE]
            odd[wi, d + 1] = plane.astype(jnp.bfloat16)
            even[wi, d + 1] = jnp.concatenate([edge, plane, edge], 0).astype(jnp.bfloat16)


def patch(even, odd, depth, tap):
    dh, dw = tap // 3 - 1, tap % 3 - 1
    if dh == 0:
        cut = odd[dw + 1, pl.ds(depth, TD)]
    else:
        lo = (dh + 1) * TW
        cut = even[dw + 1, pl.ds(depth, TD), lo:lo + PLANE]
    return cut.reshape(VOX, cut.shape[-1])


def kernel(n, nsec, plan, incoming, feed, weights, up, grad,
           w_ref, pool, upv, ea, oa, eb, ob, a_send, d_send, d_mid, a_recv, d_recv, big, acc,
           g_send, g_recv, w_sem, in_sem, up_sem, sec_s, sec_r, as_s, as_r, ar_s, ar_r,
           dz_s, dz_r, dy_s, dy_r, dm_s, dm_r, g_s, g_r):
    me = lax.axis_index("dp")
    sec = lax.axis_index("section")
    ny, nz = a_recv.shape[1:3]
    core = lax.rem(me, 2)
    y = lax.rem(me // 2, ny)
    z = me // (2 * ny)
    mate = me + 1 - 2 * core
    block = d_recv.shape[-2]
    half = block // 2
    last = sec == nsec - 1

    def at(zz, yy, cc):
        return (zz * ny + yy) * 2 + cc

    def z_of(k):
        return lax.rem(z + k, nz)

    def y_of(k):
        return lax.rem(y + k, ny)

    def up_copy(tick):
        return pltpu.make_async_copy(upv.at[tick], up.at[tick], up_sem.at[tick])

    load_in = pltpu.make_async_copy(incoming.at[0], upv.at[0], in_sem.at[0])
    load_pool = pltpu.make_async_copy(feed, pool, in_sem.at[1])
    loads = [pltpu.make_async_copy(weights.at[0, b], w_ref.at[b], w_sem.at[b]) for b in (0, 1)]
    load_in.start()
    loads[1].start()
    loads[0].start()
    load_pool.start()

    barrier = pltpu.get_barrier_semaphore()
    peers = [mate]
    peers += [at(z_of(k), y, cc) for k in range(1, nz) for cc in (0, 1)]
    peers += [at(z, y_of(k), cc) for k in range(1, ny) for cc in (0, 1)]
    for peer in peers:
        pl.semaphore_signal(barrier, inc=1, device_id={"dp": peer}, device_id_type=MESH)

    @pl.when(sec > 0)
    def _():
        pl.semaphore_signal(barrier, inc=1, device_id={"section": sec - 1}, device_id_type=MESH)

    @pl.when(sec < nsec - 1)
    def _():
        pl.semaphore_signal(barrier, inc=1, device_id={"section": sec + 1}, device_id_type=MESH)

    for wi in range(3):
        for ref in (ea, oa, eb, ob):
            for d in (0, TD + 1):
                ref[wi, d] = jnp.zeros(ref.shape[2:], jnp.bfloat16)
    load_in.wait()
    extra = jnp.where(sec > 0, 1, 0) + jnp.where(sec < nsec - 1, 1, 0)
    pl.semaphore_wait(barrier, len(peers) + extra)

    def a_direct(stage, idx, peer, to, slot):
        return pltpu.make_async_remote_copy(
            src_ref=a_send.at[stage, to], dst_ref=a_recv.at[(stage,) + slot],
            send_sem=as_s.at[stage, idx], recv_sem=as_r.at[(stage,) + slot],
            device_id={"dp": peer}, device_id_type=MESH)

    def a_relay(stage, yy, slot):
        return pltpu.make_async_remote_copy(
            src_ref=a_recv.at[(stage,) + slot], dst_ref=a_recv.at[(stage,) + slot],
            send_sem=ar_s.at[stage, yy, slot[1]], recv_sem=ar_r.at[(stage,) + slot],
            device_id={"dp": at(z, yy, core)}, device_id_type=MESH)

    def d_along_z(stage, zz, slot):
        return pltpu.make_async_remote_copy(
            src_ref=d_send.at[stage, zz], dst_ref=d_mid.at[stage, :, slot],
            send_sem=dz_s.at[stage, zz], recv_sem=dz_r.at[stage, slot],
            device_id={"dp": at(zz, y, core)}, device_id_type=MESH)

    def d_along_y(stage, yy, slot):
        return pltpu.make_async_remote_copy(
            src_ref=d_mid.at[stage, yy], dst_ref=d_recv.at[stage, core, slot],
            send_sem=dy_s.at[stage, yy], recv_sem=dy_r.at[stage, slot],
            device_id={"dp": at(z, yy, core)}, device_id_type=MESH)

    def d_to_mate(stage, whose):
        return pltpu.make_async_remote_copy(
            src_ref=d_recv.at[stage, whose], dst_ref=d_recv.at[stage, whose],
            send_sem=dm_s.at[stage], recv_sem=dm_r.at[stage],
            device_id={"dp": mate}, device_id_type=MESH)

    def directs(stage):
        mine = (y, z, core)
        out = []
        for k in range(1, nz):
            for cc in (0, 1):
                out.append(a_direct(stage, len(out), at(z_of(k), y, cc), cc, mine))
        for k in range(1, ny):
            for cc in (0, 1):
                out.append(a_direct(stage, len(out), at(z, y_of(k), cc), cc, mine))
        out.append(a_direct(stage, len(out), mate, 1 - core, mine))
        return out

    def share(stage, act, err):
        a_send[stage, 0] = act[:, :LANES]
        a_send[stage, 1] = act[:, LANES:]
        turned = jnp.transpose(err).astype(jnp.bfloat16)
        d_send[stage] = turned.reshape(d_send.shape[1:])
        for k in range(1, nz):
            d_along_z(stage, z_of(k), z).start()
        for copy in directs(stage):
            copy.start()
        a_recv[stage, y, z, core] = a_send[stage, core]
        for yy in range(ny):
            d_mid[stage, yy, z] = d_send[stage, z, yy]

    def relay(stage):
        for k in range(1, nz):
            d_along_z(stage, z, z_of(k)).wait_recv()
        for k in range(1, ny):
            d_along_y(stage, y_of(k), y).start()
        d_recv[stage, core, y] = d_mid[stage, y]
        for k in range(1, nz):
            for cc in (0, 1):
                a_direct(stage, 0, mate, 0, (y, z_of(k), cc)).wait_recv()
            for j in range(1, ny):
                a_relay(stage, y_of(j), (y, z_of(k))).start()

    def swap_errors(stage):
        for k in range(1, ny):
            d_along_y(stage, y, y_of(k)).wait_recv()
        d_to_mate(stage, core).start()

    def arrive(stage):
        a_direct(stage, 0, mate, 0, (y, z, 1 - core)).wait_recv()
        for j in range(1, ny):
            for cc in (0, 1):
                a_direct(stage, 0, mate, 0, (y_of(j), z, cc)).wait_recv()
            for k in range(1, nz):
                a_relay(stage, y, (y_of(j), z_of(k))).wait_recv()

    def sent(stage):
        for k in range(1, nz):
            d_along_z(stage, z_of(k), z).wait_send()
        for copy in directs(stage):
            copy.wait_send()
        for j in range(1, ny):
            d_along_y(stage, y_of(j), y).wait_send()
            for k in range(1, nz):
                a_relay(stage, y_of(j), (y, z_of(k))).wait_send()
        d_to_mate(stage, core).wait_send()

    def convs(b, hook):
        zero = jnp.zeros((VOX, w_ref.shape[2]), jnp.float32)

        def forward(dd, total):
            for tap in range(9):
                total += lax.dot_general(patch(ea, oa, dd, tap), w_ref[b, 9 * dd + tap],
                                         (((1,), (1,)), ((), ())), preferred_element_type=jnp.float32)
            return total

        def backward(dd, total):
            for tap in range(9):
                total += jnp.dot(patch(eb, ob, 2 - dd, 8 - tap), w_ref[b, 9 * dd + tap],
                                 preferred_element_type=jnp.float32)
            return total

        fwd = lax.fori_loop(0, 3, forward, zero)
        hook()
        bwd = lax.fori_loop(0, 3, backward, zero)
        return fwd, bwd

    def sec_copy(j):
        return pltpu.make_async_remote_copy(
            src_ref=upv.at[0, j], dst_ref=upv.at[1, j], send_sem=sec_s.at[j], recv_sem=sec_r.at[j],
            device_id={"section": lax.rem(sec + nsec - 1, nsec)}, device_id_type=MESH)

    stages = 2 * TICKS

    @pl.loop(0, stages)
    def _(stage):
        tick, p = stage // 2, lax.rem(stage, 2)

        @pl.when(stage == 2)
        def _():
            load_pool.wait()

            @pl.when(last)
            def _():
                upv[1] = pool[plan[0, 0]]

            @pl.when(sec < nsec - 1)
            def _():
                for j in range(4):
                    sec_copy(j).wait_recv()

        u = upv[tick, p].astype(jnp.float32)
        act = u * sigmoid(u)
        err = upv[tick, 3 - p].astype(jnp.float32)
        share(stage, act.astype(jnp.bfloat16), err)
        fill(ea, oa, act)
        fill(eb, ob, err)
        for b in (0, 1):
            @pl.when(stage == 1 - b)
            def _():
                loads[b].wait()

        def hook():
            @pl.when(stage > 0)
            def _():
                relay(stage - 1)

        fwd, bwd = convs(1 - p, hook)
        u = upv[tick, p].astype(jnp.float32)
        upv[tick, 1 - p] = (upv[tick, 1 - p].astype(jnp.float32) - fwd).astype(jnp.bfloat16)
        upv[tick, 2 + p] = (upv[tick, 2 + p].astype(jnp.float32) + bwd * silu_grad(u, sigmoid(u))).astype(jnp.bfloat16)

        @pl.when((stage == 0) & (sec > 0))
        def _():
            sec_copy(1).start()
            sec_copy(2).start()

        @pl.when((stage == 1) & (sec > 0))
        def _():
            sec_copy(0).start()
            sec_copy(3).start()

        @pl.when(p == 1)
        def _():
            up_copy(tick).start()

    lane = lax.broadcasted_iota(jnp.int32, (8, VOX), 1)
    masks = {}
    for step, size in ((1, TW), (TW, TH), (PLANE, TD)):
        at_axis = (lane // step) % size
        masks[step] = at_axis >= 1
        masks[-step] = at_axis < size - 1

    def moved(x, by):
        if by == 0:
            return x
        return jnp.where(masks[by], pltpu.roll(x, by % VOX, 2), 0.0)

    def g_copy(b):
        return pltpu.make_async_remote_copy(
            src_ref=g_send.at[b], dst_ref=g_recv.at[b], send_sem=g_s.at[b], recv_sem=g_r.at[b],
            device_id={"dp": mate}, device_id_type=MESH)

    tiles = 3
    per = TAPS * block // tiles
    relay(stages - 1)
    swap_errors(0)
    @pl.loop(0, stages)
    def _(stage):
        b = lax.rem(stage, 2)

        @pl.when(stage + 1 < stages)
        def _():
            swap_errors(stage + 1)

        d_to_mate(stage, 1 - core).wait_recv()
        arrive(stage)

        @pl.loop(0, n)
        def _(r):
            q = r // 2
            x = d_recv[stage, lax.rem(r, 2), q // nz, lax.rem(q, nz)]
            x = x.astype(jnp.float32).reshape(block // 8, 8, VOX)
            cols = pl.ds(pl.multiple_of(r * VOX, VOX), VOX)
            for dw in (-1, 0, 1):
                xw = moved(x, dw)
                for dh in (-1, 0, 1):
                    xh = moved(xw, dh * TW)
                    for dd in (-1, 0, 1):
                        lo = (9 * (dd + 1) + 3 * (dh + 1) + dw + 1) * block
                        s = moved(xh, dd * PLANE).reshape(block, VOX)
                        big[lo:lo + block, cols] = s.astype(jnp.bfloat16)

        @pl.loop(0, tiles)
        def _(m):
            rows = pl.ds(pl.multiple_of(m * per, 16), per)
            got = jnp.dot(big[rows, :], a_recv[stage].reshape(n * VOX, LANES),
                          preferred_element_type=jnp.float32)
            @pl.when(stage < 2)
            def _():
                acc[b, rows, :] = got

            @pl.when(stage >= 2)
            def _():
                acc[b, rows, :] += got

        @pl.when(stage >= stages - 2)
        def _():
            lo = pl.multiple_of((1 - core) * half, 8)
            for tap in range(TAPS):
                g_send[b, tap] = acc[b, pl.ds(tap * block + lo, half), :]
            g_copy(b).start()

    mine = pl.ds(pl.multiple_of(core * LANES, LANES), LANES)
    other = pl.ds(pl.multiple_of((1 - core) * LANES, LANES), LANES)
    for b in (0, 1):
        for tap in range(TAPS):
            lo = pl.multiple_of(tap * block + core * half, 8)
            grad[1 - b, tap, :, mine] = acc[b, pl.ds(lo, half), :]
    for b in (0, 1):
        g_copy(b).wait_recv()
        grad[1 - b, :, :, other] = g_recv[b]
    for b in (0, 1):
        g_copy(b).wait_send()
    @pl.loop(0, stages)
    def _(stage):
        sent(stage)

    for tick in range(TICKS):
        up_copy(tick).wait()

    @pl.when(sec > 0)
    def _():
        for j in range(4):
            sec_copy(j).wait_send()


def body(incoming, feed, plan, weights, momentum):
    n = lax.axis_size("dp")
    nsec = lax.axis_size("section")
    channels = weights.shape[-1]
    block = 2 * channels // n
    ny = max(1, n // 8)
    nz = n // (2 * ny)
    stages = 2 * TICKS
    bf, f32 = jnp.bfloat16, jnp.float32
    vm = pl.BlockSpec(memory_space=pltpu.VMEM)
    hbm = pl.BlockSpec(memory_space=pl.ANY)
    dma = pltpu.SemaphoreType.DMA
    incoming = pltpu.with_memory_space_constraint(incoming, pltpu.HBM)
    feed = pltpu.with_memory_space_constraint(feed, pltpu.HBM)
    up, grad = pl.pallas_call(
        functools.partial(kernel, n, nsec),
        out_shape=(
            jax.ShapeDtypeStruct((TICKS, 4, VOX, channels), bf),
            jax.ShapeDtypeStruct((2, TAPS, block // 2, channels), f32),
        ),
        in_specs=[pl.BlockSpec(memory_space=pltpu.SMEM)] + [pl.BlockSpec(memory_space=pltpu.HBM)] * 3,
        out_specs=(hbm, vm),
        scratch_shapes=[
            pltpu.VMEM(weights.shape[1:], bf),
            pltpu.VMEM(feed.shape, bf),
            pltpu.VMEM((TICKS, 4, VOX, channels), bf),
            pltpu.VMEM((3, TD + 2, PLANE + 2 * TW, channels), bf),
            pltpu.VMEM((3, TD + 2, PLANE, channels), bf),
            pltpu.VMEM((3, TD + 2, PLANE + 2 * TW, channels), bf),
            pltpu.VMEM((3, TD + 2, PLANE, channels), bf),
            pltpu.VMEM((stages, 2, VOX, LANES), bf),
            pltpu.VMEM((stages, nz, ny, block, VOX), bf),
            pltpu.VMEM((stages, ny, nz, block, VOX), bf),
            pltpu.VMEM((stages, ny, nz, 2, VOX, LANES), bf),
            pltpu.VMEM((stages, 2, ny, nz, block, VOX), bf),
            pltpu.VMEM((TAPS * block, n * VOX), bf),
            pltpu.VMEM((2, TAPS * block, LANES), f32),
            pltpu.VMEM((2, TAPS, block // 2, LANES), f32),
            pltpu.VMEM((2, TAPS, block // 2, LANES), f32),
            dma((2,)), dma((2,)), dma((TICKS,)), dma((4,)), dma((4,)),
            dma((stages, 2 * (ny + nz))), dma((stages, ny, nz, 2)), dma((stages, ny, nz)), dma((stages, ny, nz)),
            dma((stages, nz)), dma((stages, nz)), dma((stages, ny)), dma((stages, ny)),
            dma((stages,)), dma((stages,)), dma((2,)), dma((2,)),
        ],
        compiler_params=pltpu.CompilerParams(
            collective_id=0, has_side_effects=True, vmem_limit_bytes=48 * 1024 * 1024),
        cost_estimate=pl.CostEstimate(flops=12 * TICKS * VOX * TAPS * channels * channels,
                                      bytes_accessed=weights.size * 2, transcendentals=0),
    )(plan, incoming, feed, weights)
    new_momentum = 0.9 * momentum[0] + grad / (n * TICKS)
    return (up[:, None], new_momentum[None])


def solution(mesh):
    in_specs = (
        P("section", None, "dp", None),
        P(None, None, "dp", None),
        P(None, "dp"),
        P("section", None, None, None, None),
        P("section", None, None, "dp", None),
    )
    out_specs = (P(None, "section", None, "dp", None), P("section", None, None, "dp", None))
    return jax.shard_map(body, mesh=mesh, in_specs=in_specs, out_specs=out_specs, check_vma=False)
```

```python
import functools

import jax
import jax.numpy as jnp
from jax import lax
from jax.experimental import pallas as pl
from jax.experimental.pallas import tpu as pltpu
from jax.sharding import PartitionSpec as P

TD = 2
TH = 8
TW = 8
TICKS = 2
VOX = TD * TH * TW
PLANE = TH * TW
TAPS = 27
LANES = 128
MESH = pl.DeviceIdType.MESH


def tap_offset(tap):
    return tap // 9 - 1, (tap // 3) % 3 - 1, tap % 3 - 1


def sigmoid(u):
    return 1.0 / (1.0 + jnp.exp(-u))


def silu_grad(u, s):
    return s * (1.0 + u * (1.0 - s))


def fill(even, odd, x):
    row = lax.broadcasted_iota(jnp.int32, x.shape, 0)
    w = row % TW
    edge = jnp.zeros((TW, x.shape[1]), jnp.float32)
    for wi, dw in enumerate((-1, 0, 1)):
        s = x
        if dw:
            s = pltpu.roll(x, (-dw) % VOX, 0)
            s = jnp.where((w + dw >= 0) & (w + dw < TW), s, 0.0)
        for d in range(TD):
            plane = s[d * PLANE:(d + 1) * PLANE]
            odd[wi, d + 1] = plane.astype(jnp.bfloat16)
            even[wi, d + 1] = jnp.concatenate([edge, plane, edge], 0).astype(jnp.bfloat16)


def patch(even, odd, tap):
    dd, dh, dw = tap_offset(tap)
    if dh == 0:
        cut = odd[dw + 1, dd + 1:dd + 1 + TD]
    else:
        lo = (dh + 1) * TW
        cut = even[dw + 1, dd + 1:dd + 1 + TD, lo:lo + PLANE]
    return cut.reshape(VOX, cut.shape[-1])


def kernel(n, nsec, plan, incoming, feed, weights, up, grad,
           w_ref, first, pool, nxt, upv, ea, oa, eb, ob, a_send, d_send, d_mid, a_recv, d_recv, big, acc,
           g_send, g_recv, w_sem, in_sem, up_sem, sec_s, sec_r, as_s, as_r, ar_s, ar_r, ap_s, ap_r,
           dz_s, dz_r, dy_s, dy_r, dm_s, dm_r, g_s, g_r):
    me = lax.axis_index("dp")
    sec = lax.axis_index("section")
    ny, nz = a_recv.shape[1:3]
    core = lax.rem(me, 2)
    y = lax.rem(me // 2, ny)
    z = me // (2 * ny)
    mate = me + 1 - 2 * core
    block = d_recv.shape[-2]
    half = block // 2
    last = sec == nsec - 1

    def at(zz, yy, cc):
        return (zz * ny + yy) * 2 + cc

    def z_of(k):
        low, high = lax.rem(z, 2), z // 2
        low = 1 - low if k % 2 else low
        high = 1 - high if k // 2 else high
        return 2 * high + low

    def y_of(k):
        return lax.rem(y + k, ny)

    load_in = pltpu.make_async_copy(incoming.at[0], first, in_sem.at[0])
    load_pool = pltpu.make_async_copy(feed, pool, in_sem.at[1])
    loads = [pltpu.make_async_copy(weights.at[0, b], w_ref.at[b], w_sem.at[b]) for b in (0, 1)]
    load_in.start()
    loads[1].start()
    loads[0].start()
    load_pool.start()

    barrier = pltpu.get_barrier_semaphore()
    peers = [mate]
    peers += [at(z_of(k), y, cc) for k in range(1, nz) for cc in (0, 1)]
    peers += [at(z, y_of(k), cc) for k in range(1, ny) for cc in (0, 1)]
    for peer in peers:
        pl.semaphore_signal(barrier, inc=1, device_id={"dp": peer}, device_id_type=MESH)

    @pl.when(sec > 0)
    def _():
        pl.semaphore_signal(barrier, inc=1, device_id={"section": sec - 1}, device_id_type=MESH)

    @pl.when(sec < nsec - 1)
    def _():
        pl.semaphore_signal(barrier, inc=1, device_id={"section": sec + 1}, device_id_type=MESH)

    for wi in range(3):
        for ref in (ea, oa, eb, ob):
            for d in (0, TD + 1):
                ref[wi, d] = jnp.zeros(ref.shape[2:], jnp.bfloat16)
    load_in.wait()
    extra = jnp.where(sec > 0, 1, 0) + jnp.where(sec < nsec - 1, 1, 0)
    pl.semaphore_wait(barrier, len(peers) + extra)

    def a_direct(stage, idx, peer, to, slot):
        return pltpu.make_async_remote_copy(
            src_ref=a_send.at[stage, to], dst_ref=a_recv.at[(stage,) + slot],
            send_sem=as_s.at[stage, idx], recv_sem=as_r.at[(stage,) + slot],
            device_id={"dp": peer}, device_id_type=MESH)

    def a_relay(stage, yy, slot):
        return pltpu.make_async_remote_copy(
            src_ref=a_recv.at[(stage,) + slot], dst_ref=a_recv.at[(stage,) + slot],
            send_sem=ar_s.at[stage, yy, slot[1]], recv_sem=ar_r.at[(stage,) + slot],
            device_id={"dp": at(z, yy, core)}, device_id_type=MESH)

    def d_along_z(stage, zz, slot):
        return pltpu.make_async_remote_copy(
            src_ref=d_send.at[stage, zz], dst_ref=d_mid.at[stage, :, slot],
            send_sem=dz_s.at[stage, zz], recv_sem=dz_r.at[stage, slot],
            device_id={"dp": at(zz, y, core)}, device_id_type=MESH)

    def d_along_y(stage, yy, slot):
        return pltpu.make_async_remote_copy(
            src_ref=d_mid.at[stage, yy], dst_ref=d_recv.at[stage, core, slot],
            send_sem=dy_s.at[stage, yy], recv_sem=dy_r.at[stage, slot],
            device_id={"dp": at(z, yy, core)}, device_id_type=MESH)

    def d_to_mate(stage, whose):
        return pltpu.make_async_remote_copy(
            src_ref=d_recv.at[stage, whose], dst_ref=d_recv.at[stage, whose],
            send_sem=dm_s.at[stage], recv_sem=dm_r.at[stage],
            device_id={"dp": mate}, device_id_type=MESH)

    def directs(stage):
        mine = (y, z, core)
        out = []
        for k in (1, 2):
            for cc in (0, 1):
                out.append(a_direct(stage, len(out), at(z_of(k), y, cc), cc, mine))
        for k in range(1, ny):
            for cc in (0, 1):
                out.append(a_direct(stage, len(out), at(z, y_of(k), cc), cc, mine))
        out.append(a_direct(stage, len(out), mate, 1 - core, mine))
        return out

    def share(stage, act, err):
        a_send[stage, 0] = act[:, :LANES]
        a_send[stage, 1] = act[:, LANES:]
        turned = jnp.transpose(err).astype(jnp.bfloat16)
        d_send[stage] = turned.reshape(d_send.shape[1:])
        for k in range(1, nz):
            d_along_z(stage, z_of(k), z).start()
        for copy in directs(stage):
            copy.start()
        a_recv[stage, y, z, core] = a_send[stage, core]
        for yy in range(ny):
            d_mid[stage, yy, z] = d_send[stage, z, yy]

    def pass_on(stage, slot):
        return pltpu.make_async_remote_copy(
            src_ref=a_recv.at[stage, y, slot], dst_ref=a_recv.at[stage, y, slot],
            send_sem=ap_s.at[stage], recv_sem=ap_r.at[stage],
            device_id={"dp": at(z_of(1), y, core)}, device_id_type=MESH)

    def relay_near(stage):
        for cc in (0, 1):
            a_direct(stage, 0, mate, 0, (y, z_of(2), cc)).wait_recv()
        pass_on(stage, z_of(2)).start()
        for j in range(1, ny):
            a_relay(stage, y_of(j), (y, z_of(2))).start()
        for cc in (0, 1):
            a_direct(stage, 0, mate, 0, (y, z_of(1), cc)).wait_recv()
        for j in range(1, ny):
            a_relay(stage, y_of(j), (y, z_of(1))).start()

    def relay_far(stage):
        for k in range(1, nz):
            d_along_z(stage, z, z_of(k)).wait_recv()
        for k in range(1, ny):
            d_along_y(stage, y_of(k), y).start()
        d_recv[stage, core, y] = d_mid[stage, y]
        pass_on(stage, z_of(3)).wait_recv()
        for j in range(1, ny):
            a_relay(stage, y_of(j), (y, z_of(3))).start()

    def swap_errors(stage):
        for k in range(1, ny):
            d_along_y(stage, y, y_of(k)).wait_recv()
        d_to_mate(stage, core).start()

    def arrive(stage):
        a_direct(stage, 0, mate, 0, (y, z, 1 - core)).wait_recv()
        for j in range(1, ny):
            for cc in (0, 1):
                a_direct(stage, 0, mate, 0, (y_of(j), z, cc)).wait_recv()
            for k in range(1, nz):
                a_relay(stage, y, (y_of(j), z_of(k))).wait_recv()

    def sent(stage):
        for k in range(1, nz):
            d_along_z(stage, z_of(k), z).wait_send()
        for copy in directs(stage):
            copy.wait_send()
        for j in range(1, ny):
            d_along_y(stage, y_of(j), y).wait_send()
            for k in range(1, nz):
                a_relay(stage, y_of(j), (y, z_of(k))).wait_send()
        pass_on(stage, z_of(2)).wait_send()
        d_to_mate(stage, core).wait_send()

    def convs(b, near, far):
        near()
        fwd = jnp.zeros((VOX, w_ref.shape[2]), jnp.float32)
        for tap in range(TAPS):
            fwd += lax.dot_general(patch(ea, oa, tap), w_ref[b, tap], (((1,), (1,)), ((), ())),
                                   preferred_element_type=jnp.float32)
        far()
        bwd = jnp.zeros((VOX, w_ref.shape[3]), jnp.float32)
        for tap in range(TAPS):
            bwd += jnp.dot(patch(eb, ob, TAPS - 1 - tap), w_ref[b, tap],
                           preferred_element_type=jnp.float32)
        return fwd, bwd

    def sec_copy(j):
        return pltpu.make_async_remote_copy(
            src_ref=upv.at[0, j], dst_ref=nxt.at[j], send_sem=sec_s.at[j], recv_sem=sec_r.at[j],
            device_id={"section": lax.rem(sec + nsec - 1, nsec)}, device_id_type=MESH)

    for tick in range(TICKS):
        if tick == 0:
            cur = first
        else:
            cur = nxt
            load_pool.wait()

            @pl.when(last)
            def _():
                nxt[...] = pool[plan[0, 0]]

            @pl.when(sec < nsec - 1)
            def _():
                for j in range(4):
                    sec_copy(j).wait_recv()
        y1 = cur[0].astype(jnp.float32)
        s1 = sigmoid(y1)
        a1 = y1 * s1
        dy2 = cur[3].astype(jnp.float32)
        share(2 * tick, a1.astype(jnp.bfloat16), dy2)
        fill(ea, oa, a1)
        fill(eb, ob, dy2)
        if tick == 0:
            loads[1].wait()
        fwd, bwd = convs(1, lambda: relay_near(1) if tick else None, lambda: relay_far(1) if tick else None)
        x2 = (cur[1].astype(jnp.float32) - fwd).astype(jnp.bfloat16)
        dx1 = (cur[2].astype(jnp.float32) + bwd * silu_grad(y1, s1)).astype(jnp.bfloat16)
        upv[tick, 1] = x2
        upv[tick, 2] = dx1
        if tick == 0:
            @pl.when(sec > 0)
            def _():
                sec_copy(1).start()
                sec_copy(2).start()
        u = x2.astype(jnp.float32)
        s2 = sigmoid(u)
        a2 = u * s2
        e1 = dx1.astype(jnp.float32)
        share(2 * tick + 1, a2.astype(jnp.bfloat16), e1)
        fill(ea, oa, a2)
        fill(eb, ob, e1)
        if tick == 0:
            loads[0].wait()
        fwd, bwd = convs(0, lambda: relay_near(2 * tick), lambda: relay_far(2 * tick))
        u = upv[tick, 1].astype(jnp.float32)
        s2 = sigmoid(u)
        upv[tick, 0] = (cur[0].astype(jnp.float32) - fwd).astype(jnp.bfloat16)
        upv[tick, 3] = (cur[3].astype(jnp.float32) + bwd * silu_grad(u, s2)).astype(jnp.bfloat16)
        if tick == 0:
            @pl.when(sec > 0)
            def _():
                sec_copy(0).start()
                sec_copy(3).start()
        pltpu.make_async_copy(upv.at[tick], up.at[tick], up_sem.at[tick]).start()

    lane = lax.broadcasted_iota(jnp.int32, (8, VOX), 1)
    masks = {}
    for step, size in ((1, TW), (TW, TH), (PLANE, TD)):
        at_axis = (lane // step) % size
        masks[step] = at_axis >= 1
        masks[-step] = at_axis < size - 1

    def moved(x, by):
        if by == 0:
            return x
        return jnp.where(masks[by], pltpu.roll(x, by % VOX, 2), 0.0)

    def g_copy(b):
        return pltpu.make_async_remote_copy(
            src_ref=g_send.at[b], dst_ref=g_recv.at[b], send_sem=g_s.at[b], recv_sem=g_r.at[b],
            device_id={"dp": mate}, device_id_type=MESH)

    tiles = 3
    per = TAPS * block // tiles
    stages = 2 * TICKS
    relay_near(stages - 1)
    swap_errors(0)
    for stage in range(stages):
        b = stage % 2
        if stage == 1:
            relay_far(stages - 1)
        if stage + 1 < stages:
            swap_errors(stage + 1)
        d_to_mate(stage, 1 - core).wait_recv()
        arrive(stage)

        @pl.loop(0, n // 2)
        def _(r):
            yy, zz = r // nz, lax.rem(r, nz)
            for cc in (0, 1):
                x = d_recv[stage, cc, yy, zz].astype(jnp.float32).reshape(block // 8, 8, VOX)
                cols = pl.ds(pl.multiple_of((2 * r + cc) * VOX, VOX), VOX)
                for dw in (-1, 0, 1):
                    xw = moved(x, dw)
                    for dh in (-1, 0, 1):
                        xh = moved(xw, dh * TW)
                        for dd in (-1, 0, 1):
                            lo = (9 * (dd + 1) + 3 * (dh + 1) + dw + 1) * block
                            s = moved(xh, dd * PLANE).reshape(block, VOX)
                            big[lo:lo + block, cols] = s.astype(jnp.bfloat16)

        @pl.loop(0, tiles)
        def _(m):
            rows = pl.ds(pl.multiple_of(m * per, 16), per)
            got = jnp.dot(big[rows, :], a_recv[stage].reshape(n * VOX, LANES),
                          preferred_element_type=jnp.float32)
            if stage < 2:
                acc[b, rows, :] = got
            else:
                acc[b, rows, :] += got
        if stage >= 2 * TICKS - 2:
            view = acc.at[b]
            for tap in range(TAPS):
                lo = pl.multiple_of(tap * block + (1 - core) * half, 8)
                g_send[b, tap] = view[pl.ds(lo, half), :]
            g_copy(b).start()
    mine = pl.ds(pl.multiple_of(core * LANES, LANES), LANES)
    other = pl.ds(pl.multiple_of((1 - core) * LANES, LANES), LANES)
    for b in (0, 1):
        for tap in range(TAPS):
            lo = pl.multiple_of(tap * block + core * half, 8)
            grad[1 - b, tap, :, mine] = acc[b, pl.ds(lo, half), :]
    for b in (0, 1):
        g_copy(b).wait_recv()
        grad[1 - b, :, :, other] = g_recv[b]
    for b in (0, 1):
        g_copy(b).wait_send()
    @pl.loop(0, stages)
    def _(stage):
        sent(stage)

    for tick in range(TICKS):
        pltpu.make_async_copy(upv.at[tick], up.at[tick], up_sem.at[tick]).wait()

    @pl.when(sec > 0)
    def _():
        for j in range(4):
            sec_copy(j).wait_send()


def body(incoming, feed, plan, weights, momentum):
    n = lax.axis_size("dp")
    nsec = lax.axis_size("section")
    channels = weights.shape[-1]
    block = 2 * channels // n
    ny = max(1, n // 8)
    nz = n // (2 * ny)
    stages = 2 * TICKS
    bf, f32 = jnp.bfloat16, jnp.float32
    vm = pl.BlockSpec(memory_space=pltpu.VMEM)
    hbm = pl.BlockSpec(memory_space=pl.ANY)
    dma = pltpu.SemaphoreType.DMA
    incoming = pltpu.with_memory_space_constraint(incoming, pltpu.HBM)
    feed = pltpu.with_memory_space_constraint(feed, pltpu.HBM)
    up, grad = pl.pallas_call(
        functools.partial(kernel, n, nsec),
        out_shape=(
            jax.ShapeDtypeStruct((TICKS, 4, VOX, channels), bf),
            jax.ShapeDtypeStruct((2, TAPS, block // 2, channels), f32),
        ),
        in_specs=[pl.BlockSpec(memory_space=pltpu.SMEM)] + [pl.BlockSpec(memory_space=pltpu.HBM)] * 3,
        out_specs=(hbm, vm),
        scratch_shapes=[
            pltpu.VMEM(weights.shape[1:], bf),
            pltpu.VMEM((4, VOX, channels), bf),
            pltpu.VMEM(feed.shape, bf),
            pltpu.VMEM((4, VOX, channels), bf),
            pltpu.VMEM((TICKS, 4, VOX, channels), bf),
            pltpu.VMEM((3, TD + 2, PLANE + 2 * TW, channels), bf),
            pltpu.VMEM((3, TD + 2, PLANE, channels), bf),
            pltpu.VMEM((3, TD + 2, PLANE + 2 * TW, channels), bf),
            pltpu.VMEM((3, TD + 2, PLANE, channels), bf),
            pltpu.VMEM((stages, 2, VOX, LANES), bf),
            pltpu.VMEM((stages, nz, ny, block, VOX), bf),
            pltpu.VMEM((stages, ny, nz, block, VOX), bf),
            pltpu.VMEM((stages, ny, nz, 2, VOX, LANES), bf),
            pltpu.VMEM((stages, 2, ny, nz, block, VOX), bf),
            pltpu.VMEM((TAPS * block, n * VOX), bf),
            pltpu.VMEM((2, TAPS * block, LANES), f32),
            pltpu.VMEM((2, TAPS, block // 2, LANES), f32),
            pltpu.VMEM((2, TAPS, block // 2, LANES), f32),
            dma((2,)), dma((2,)), dma((TICKS,)), dma((4,)), dma((4,)),
            dma((stages, 2 * (ny + nz))), dma((stages, ny, nz, 2)), dma((stages, ny, nz)), dma((stages, ny, nz)),
            dma((stages,)), dma((stages,)),
            dma((stages, nz)), dma((stages, nz)), dma((stages, ny)), dma((stages, ny)),
            dma((stages,)), dma((stages,)), dma((2,)), dma((2,)),
        ],
        compiler_params=pltpu.CompilerParams(
            collective_id=0, has_side_effects=True, vmem_limit_bytes=48 * 1024 * 1024),
        cost_estimate=pl.CostEstimate(flops=12 * TICKS * VOX * TAPS * channels * channels,
                                      bytes_accessed=weights.size * 2, transcendentals=0),
    )(plan, incoming, feed, weights)
    new_momentum = 0.9 * momentum[0] + grad / (n * TICKS)
    return (up[:, None], new_momentum[None])


def solution(mesh):
    in_specs = (
        P("section", None, "dp", None),
        P(None, None, "dp", None),
        P(None, "dp"),
        P("section", None, None, None, None),
        P("section", None, None, "dp", None),
    )
    out_specs = (P(None, "section", None, "dp", None), P("section", None, None, "dp", None))
    return jax.shard_map(body, mesh=mesh, in_specs=in_specs, out_specs=out_specs, check_vma=False)
```

```python
import functools

import jax
import jax.numpy as jnp
from jax import lax
from jax.experimental import pallas as pl
from jax.experimental.pallas import tpu as pltpu
from jax.sharding import PartitionSpec as P

TD = 2
TH = 8
TW = 8
TICKS = 2
VOX = TD * TH * TW
PLANE = TH * TW
TAPS = 27
LANES = 128
MESH = pl.DeviceIdType.MESH


def tap_offset(tap):
    return tap // 9 - 1, (tap // 3) % 3 - 1, tap % 3 - 1


def sigmoid(u):
    return 1.0 / (1.0 + jnp.exp(-u))


def silu_grad(u, s):
    return s * (1.0 + u * (1.0 - s))


def fill(even, odd, x):
    row = lax.broadcasted_iota(jnp.int32, x.shape, 0)
    w = row % TW
    edge = jnp.zeros((TW, x.shape[1]), jnp.float32)
    for wi, dw in enumerate((-1, 0, 1)):
        s = x
        if dw:
            s = pltpu.roll(x, (-dw) % VOX, 0)
            s = jnp.where((w + dw >= 0) & (w + dw < TW), s, 0.0)
        for d in range(TD):
            plane = s[d * PLANE:(d + 1) * PLANE]
            odd[wi, d + 1] = plane.astype(jnp.bfloat16)
            even[wi, d + 1] = jnp.concatenate([edge, plane, edge], 0).astype(jnp.bfloat16)


def patch(even, odd, tap):
    dd, dh, dw = tap_offset(tap)
    if dh == 0:
        cut = odd[dw + 1, dd + 1:dd + 1 + TD]
    else:
        lo = (dh + 1) * TW
        cut = even[dw + 1, dd + 1:dd + 1 + TD, lo:lo + PLANE]
    return cut.reshape(VOX, cut.shape[-1])


def kernel(n, nsec, plan, incoming, feed, weights, up, grad,
           w_ref, first, pool, nxt, upv, ea, oa, eb, ob, a_send, d_send, d_mid, a_recv, d_recv, big, acc,
           w_sem, in_sem, up_sem, sec_s, sec_r, as_s, as_r, ar_s, ar_r, ap_s, ap_r,
           dz_s, dz_r, dy_s, dy_r, dm_s, dm_r, mp_s, mp_r):
    me = lax.axis_index("dp")
    sec = lax.axis_index("section")
    ny, nz = a_recv.shape[2:4]
    core = lax.rem(me, 2)
    y = lax.rem(me // 2, ny)
    z = me // (2 * ny)
    mate = me + 1 - 2 * core
    block = d_recv.shape[-2]
    half = block // 2
    last = sec == nsec - 1

    def at(zz, yy, cc):
        return (zz * ny + yy) * 2 + cc

    def z_of(k):
        low, high = lax.rem(z, 2), z // 2
        low = 1 - low if k % 2 else low
        high = 1 - high if k // 2 else high
        return 2 * high + low

    def y_of(k):
        return lax.rem(y + k, ny)

    load_in = pltpu.make_async_copy(incoming.at[0], first, in_sem.at[0])
    load_pool = pltpu.make_async_copy(feed, pool, in_sem.at[1])
    loads = [pltpu.make_async_copy(weights.at[0, b], w_ref.at[b], w_sem.at[b]) for b in (0, 1)]
    load_in.start()
    loads[1].start()
    loads[0].start()
    load_pool.start()

    barrier = pltpu.get_barrier_semaphore()
    peers = [mate]
    peers += [at(z_of(k), y, cc) for k in range(1, nz) for cc in (0, 1)]
    peers += [at(z, y_of(k), cc) for k in range(1, ny) for cc in (0, 1)]
    for peer in peers:
        pl.semaphore_signal(barrier, inc=1, device_id={"dp": peer}, device_id_type=MESH)

    @pl.when(sec > 0)
    def _():
        pl.semaphore_signal(barrier, inc=1, device_id={"section": sec - 1}, device_id_type=MESH)

    @pl.when(sec < nsec - 1)
    def _():
        pl.semaphore_signal(barrier, inc=1, device_id={"section": sec + 1}, device_id_type=MESH)

    for wi in range(3):
        for ref in (ea, oa, eb, ob):
            for d in (0, TD + 1):
                ref[wi, d] = jnp.zeros(ref.shape[2:], jnp.bfloat16)
    load_in.wait()
    extra = jnp.where(sec > 0, 1, 0) + jnp.where(sec < nsec - 1, 1, 0)
    pl.semaphore_wait(barrier, len(peers) + extra)

    def a_direct(stage, idx, peer, to, slot):
        return pltpu.make_async_remote_copy(
            src_ref=a_send.at[stage, to], dst_ref=a_recv.at[(stage, to) + slot],
            send_sem=as_s.at[stage, idx], recv_sem=as_r.at[(stage,) + slot],
            device_id={"dp": peer}, device_id_type=MESH)

    def a_relay(stage, yy, slot):
        return pltpu.make_async_remote_copy(
            src_ref=a_recv.at[(stage, core) + slot], dst_ref=a_recv.at[(stage, core) + slot],
            send_sem=ar_s.at[stage, yy, slot[1]], recv_sem=ar_r.at[(stage,) + slot],
            device_id={"dp": at(z, yy, core)}, device_id_type=MESH)

    def d_along_z(stage, zz, slot):
        return pltpu.make_async_remote_copy(
            src_ref=d_send.at[stage, zz], dst_ref=d_mid.at[stage, :, slot],
            send_sem=dz_s.at[stage, zz], recv_sem=dz_r.at[stage, slot],
            device_id={"dp": at(zz, y, core)}, device_id_type=MESH)

    def d_along_y(stage, yy, slot):
        return pltpu.make_async_remote_copy(
            src_ref=d_mid.at[stage, yy], dst_ref=d_recv.at[stage, core, slot],
            send_sem=dy_s.at[stage, yy], recv_sem=dy_r.at[stage, slot],
            device_id={"dp": at(z, yy, core)}, device_id_type=MESH)

    def d_to_mate(stage, whose):
        return pltpu.make_async_remote_copy(
            src_ref=d_recv.at[stage, whose], dst_ref=d_recv.at[stage, whose],
            send_sem=dm_s.at[stage], recv_sem=dm_r.at[stage],
            device_id={"dp": mate}, device_id_type=MESH)

    def directs(stage):
        mine = (y, z, core)
        out = []
        for k in (1, 2):
            for cc in (0, 1):
                out.append(a_direct(stage, len(out), at(z_of(k), y, cc), cc, mine))
        for k in range(1, ny):
            for cc in (0, 1):
                out.append(a_direct(stage, len(out), at(z, y_of(k), cc), cc, mine))
        out.append(a_direct(stage, len(out), mate, 1 - core, mine))
        return out

    def share(stage, act, err):
        a_send[stage, 0] = act[:, :LANES]
        a_send[stage, 1] = act[:, LANES:]
        turned = jnp.transpose(err).astype(jnp.bfloat16)
        d_send[stage] = turned.reshape(d_send.shape[1:])
        for k in range(1, nz):
            d_along_z(stage, z_of(k), z).start()
        for copy in directs(stage):
            copy.start()
        a_recv[stage, core, y, z, core] = a_send[stage, core]
        for yy in range(ny):
            d_mid[stage, yy, z] = d_send[stage, z, yy]

    def pass_on(stage, slot):
        return pltpu.make_async_remote_copy(
            src_ref=a_recv.at[stage, core, y, slot], dst_ref=a_recv.at[stage, core, y, slot],
            send_sem=ap_s.at[stage], recv_sem=ap_r.at[stage],
            device_id={"dp": at(z_of(1), y, core)}, device_id_type=MESH)

    def a_to_mate(stage, whose, yy):
        return pltpu.make_async_remote_copy(
            src_ref=a_recv.at[stage, whose, yy], dst_ref=a_recv.at[stage, whose, yy],
            send_sem=mp_s.at[stage, yy], recv_sem=mp_r.at[stage, yy],
            device_id={"dp": mate}, device_id_type=MESH)

    def relay_near(stage):
        for cc in (0, 1):
            a_direct(stage, 0, mate, 0, (y, z_of(2), cc)).wait_recv()
        pass_on(stage, z_of(2)).start()
        for j in range(1, ny):
            a_relay(stage, y_of(j), (y, z_of(2))).start()
        for cc in (0, 1):
            a_direct(stage, 0, mate, 0, (y, z_of(1), cc)).wait_recv()
        for j in range(1, ny):
            a_relay(stage, y_of(j), (y, z_of(1))).start()

    def relay_far(stage):
        for k in range(1, nz):
            d_along_z(stage, z, z_of(k)).wait_recv()
        for k in range(1, ny):
            d_along_y(stage, y_of(k), y).start()
        d_recv[stage, core, y] = d_mid[stage, y]
        pass_on(stage, z_of(3)).wait_recv()
        for j in range(1, ny):
            a_relay(stage, y_of(j), (y, z_of(3))).start()
        a_direct(stage, 0, mate, 0, (y, z, 1 - core)).wait_recv()
        a_to_mate(stage, core, y).start()

    def swap_errors(stage):
        for k in range(1, ny):
            d_along_y(stage, y, y_of(k)).wait_recv()
        d_to_mate(stage, core).start()

    def arrive(stage):
        for j in range(1, ny):
            for cc in (0, 1):
                a_direct(stage, 0, mate, 0, (y_of(j), z, cc)).wait_recv()
            for k in range(1, nz):
                a_relay(stage, y, (y_of(j), z_of(k))).wait_recv()
            a_to_mate(stage, core, y_of(j)).start()

    def mate_arrives(stage):
        for j in range(ny):
            a_to_mate(stage, 1 - core, y_of(j)).wait_recv()

    def sent(stage):
        for k in range(1, nz):
            d_along_z(stage, z_of(k), z).wait_send()
        for copy in directs(stage):
            copy.wait_send()
        for j in range(1, ny):
            d_along_y(stage, y_of(j), y).wait_send()
            for k in range(1, nz):
                a_relay(stage, y_of(j), (y, z_of(k))).wait_send()
        pass_on(stage, z_of(2)).wait_send()
        for j in range(ny):
            a_to_mate(stage, core, y_of(j)).wait_send()
        d_to_mate(stage, core).wait_send()

    def convs(b, near, far):
        near()
        fwd = jnp.zeros((VOX, w_ref.shape[2]), jnp.float32)
        for tap in range(TAPS):
            fwd += lax.dot_general(patch(ea, oa, tap), w_ref[b, tap], (((1,), (1,)), ((), ())),
                                   preferred_element_type=jnp.float32)
        far()
        bwd = jnp.zeros((VOX, w_ref.shape[3]), jnp.float32)
        for tap in range(TAPS):
            bwd += jnp.dot(patch(eb, ob, TAPS - 1 - tap), w_ref[b, tap],
                           preferred_element_type=jnp.float32)
        return fwd, bwd

    def sec_copy(j):
        return pltpu.make_async_remote_copy(
            src_ref=upv.at[0, j], dst_ref=nxt.at[j], send_sem=sec_s.at[j], recv_sem=sec_r.at[j],
            device_id={"section": lax.rem(sec + nsec - 1, nsec)}, device_id_type=MESH)

    for tick in range(TICKS):
        if tick == 0:
            cur = first
        else:
            cur = nxt
            load_pool.wait()

            @pl.when(last)
            def _():
                nxt[...] = pool[plan[0, 0]]

            @pl.when(sec < nsec - 1)
            def _():
                for j in range(4):
                    sec_copy(j).wait_recv()
        y1 = cur[0].astype(jnp.float32)
        s1 = sigmoid(y1)
        a1 = y1 * s1
        dy2 = cur[3].astype(jnp.float32)
        share(2 * tick, a1.astype(jnp.bfloat16), dy2)
        fill(ea, oa, a1)
        fill(eb, ob, dy2)
        if tick == 0:
            loads[1].wait()
        fwd, bwd = convs(1, lambda: relay_near(1) if tick else None, lambda: relay_far(1) if tick else None)
        x2 = (cur[1].astype(jnp.float32) - fwd).astype(jnp.bfloat16)
        dx1 = (cur[2].astype(jnp.float32) + bwd * silu_grad(y1, s1)).astype(jnp.bfloat16)
        upv[tick, 1] = x2
        upv[tick, 2] = dx1
        if tick == 0:
            @pl.when(sec > 0)
            def _():
                sec_copy(1).start()
                sec_copy(2).start()
        u = x2.astype(jnp.float32)
        s2 = sigmoid(u)
        a2 = u * s2
        e1 = dx1.astype(jnp.float32)
        share(2 * tick + 1, a2.astype(jnp.bfloat16), e1)
        fill(ea, oa, a2)
        fill(eb, ob, e1)
        if tick == 0:
            loads[0].wait()
        fwd, bwd = convs(0, lambda: relay_near(2 * tick), lambda: relay_far(2 * tick))
        u = upv[tick, 1].astype(jnp.float32)
        s2 = sigmoid(u)
        upv[tick, 0] = (cur[0].astype(jnp.float32) - fwd).astype(jnp.bfloat16)
        upv[tick, 3] = (cur[3].astype(jnp.float32) + bwd * silu_grad(u, s2)).astype(jnp.bfloat16)
        if tick == 0:
            @pl.when(sec > 0)
            def _():
                sec_copy(0).start()
                sec_copy(3).start()
        pltpu.make_async_copy(upv.at[tick], up.at[tick], up_sem.at[tick]).start()

    lane = lax.broadcasted_iota(jnp.int32, (8, VOX), 1)
    masks = {}
    for step, size in ((1, TW), (TW, TH), (PLANE, TD)):
        at_axis = (lane // step) % size
        masks[step] = at_axis >= 1
        masks[-step] = at_axis < size - 1

    def moved(x, by):
        if by == 0:
            return x
        return jnp.where(masks[by], pltpu.roll(x, by % VOX, 2), 0.0)

    stages = 2 * TICKS
    depth = n * VOX
    relay_near(stages - 1)
    swap_errors(0)
    for stage in range(stages):
        b = stage % 2
        if stage == 1:
            relay_far(stages - 1)
        if stage + 1 < stages:
            swap_errors(stage + 1)
        d_to_mate(stage, 1 - core).wait_recv()
        arrive(stage)

        @pl.loop(0, n // 2)
        def _(r):
            yy, zz = r // nz, lax.rem(r, nz)
            for cc in (0, 1):
                x = d_recv[stage, cc, yy, zz].astype(jnp.float32)
                x = jnp.where(core == 0, x[:half], x[half:]).reshape(half // 8, 8, VOX)
                cols = pl.ds(pl.multiple_of((2 * r + cc) * VOX, VOX), VOX)
                rows = [None] * TAPS
                for dw in (-1, 0, 1):
                    xw = moved(x, dw)
                    for dh in (-1, 0, 1):
                        xh = moved(xw, dh * TW)
                        for dd in (-1, 0, 1):
                            tap = 9 * (dd + 1) + 3 * (dh + 1) + dw + 1
                            rows[tap] = moved(xh, dd * PLANE).reshape(half, VOX)
                big[:, cols] = jnp.concatenate(rows, 0).astype(jnp.bfloat16)

        mate_arrives(stage)
        both = jnp.concatenate([a_recv[stage, 0].reshape(depth, LANES),
                                a_recv[stage, 1].reshape(depth, LANES)], 1)
        got = jnp.dot(big[...], both, preferred_element_type=jnp.float32)
        if stage < 2:
            acc[b] = got
        else:
            grad[1 - b] = (acc[b] + got).reshape(TAPS, half, 2 * LANES)

    @pl.loop(0, stages)
    def _(stage):
        sent(stage)

    for tick in range(TICKS):
        pltpu.make_async_copy(upv.at[tick], up.at[tick], up_sem.at[tick]).wait()

    @pl.when(sec > 0)
    def _():
        for j in range(4):
            sec_copy(j).wait_send()


def body(incoming, feed, plan, weights, momentum):
    n = lax.axis_size("dp")
    nsec = lax.axis_size("section")
    channels = weights.shape[-1]
    block = 2 * channels // n
    ny = max(1, n // 8)
    nz = n // (2 * ny)
    stages = 2 * TICKS
    bf, f32 = jnp.bfloat16, jnp.float32
    vm = pl.BlockSpec(memory_space=pltpu.VMEM)
    hbm = pl.BlockSpec(memory_space=pl.ANY)
    dma = pltpu.SemaphoreType.DMA
    incoming = pltpu.with_memory_space_constraint(incoming, pltpu.HBM)
    feed = pltpu.with_memory_space_constraint(feed, pltpu.HBM)
    up, grad = pl.pallas_call(
        functools.partial(kernel, n, nsec),
        out_shape=(
            jax.ShapeDtypeStruct((TICKS, 4, VOX, channels), bf),
            jax.ShapeDtypeStruct((2, TAPS, block // 2, channels), f32),
        ),
        in_specs=[pl.BlockSpec(memory_space=pltpu.SMEM)] + [pl.BlockSpec(memory_space=pltpu.HBM)] * 3,
        out_specs=(hbm, vm),
        scratch_shapes=[
            pltpu.VMEM(weights.shape[1:], bf),
            pltpu.VMEM((4, VOX, channels), bf),
            pltpu.VMEM(feed.shape, bf),
            pltpu.VMEM((4, VOX, channels), bf),
            pltpu.VMEM((TICKS, 4, VOX, channels), bf),
            pltpu.VMEM((3, TD + 2, PLANE + 2 * TW, channels), bf),
            pltpu.VMEM((3, TD + 2, PLANE, channels), bf),
            pltpu.VMEM((3, TD + 2, PLANE + 2 * TW, channels), bf),
            pltpu.VMEM((3, TD + 2, PLANE, channels), bf),
            pltpu.VMEM((stages, 2, VOX, LANES), bf),
            pltpu.VMEM((stages, nz, ny, block, VOX), bf),
            pltpu.VMEM((stages, ny, nz, block, VOX), bf),
            pltpu.VMEM((stages, 2, ny, nz, 2, VOX, LANES), bf),
            pltpu.VMEM((stages, 2, ny, nz, block, VOX), bf),
            pltpu.VMEM((TAPS * block // 2, n * VOX), bf),
            pltpu.VMEM((2, TAPS * block // 2, channels), f32),
            dma((2,)), dma((2,)), dma((TICKS,)), dma((4,)), dma((4,)),
            dma((stages, 2 * (ny + nz))), dma((stages, ny, nz, 2)), dma((stages, ny, nz)), dma((stages, ny, nz)),
            dma((stages,)), dma((stages,)),
            dma((stages, nz)), dma((stages, nz)), dma((stages, ny)), dma((stages, ny)),
            dma((stages,)), dma((stages,)), dma((stages, ny)), dma((stages, ny)),
        ],
        compiler_params=pltpu.CompilerParams(
            collective_id=0, has_side_effects=True, vmem_limit_bytes=48 * 1024 * 1024),
        cost_estimate=pl.CostEstimate(flops=12 * TICKS * VOX * TAPS * channels * channels,
                                      bytes_accessed=weights.size * 2, transcendentals=0),
    )(plan, incoming, feed, weights)
    new_momentum = 0.9 * momentum[0] + grad / (n * TICKS)
    return (up[:, None], new_momentum[None])


def solution(mesh):
    in_specs = (
        P("section", None, "dp", None),
        P(None, None, "dp", None),
        P(None, "dp"),
        P("section", None, None, None, None),
        P("section", None, None, "dp", None),
    )
    out_specs = (P(None, "section", None, "dp", None), P("section", None, None, "dp", None))
    return jax.shard_map(body, mesh=mesh, in_specs=in_specs, out_specs=out_specs, check_vma=False)
```

```python
import functools

import jax
import jax.numpy as jnp
from jax import lax
from jax.experimental import pallas as pl
from jax.experimental.pallas import tpu as pltpu
from jax.sharding import PartitionSpec as P

TD = 2
TH = 8
TW = 8
TICKS = 2
VOX = TD * TH * TW
PLANE = TH * TW
TAPS = 27
LANES = 128
MESH = pl.DeviceIdType.MESH


def tap_offset(tap):
    return tap // 9 - 1, (tap // 3) % 3 - 1, tap % 3 - 1


def sigmoid(u):
    return 1.0 / (1.0 + jnp.exp(-u))


def silu_grad(u, s):
    return s * (1.0 + u * (1.0 - s))


def fill(even, odd, x):
    row = lax.broadcasted_iota(jnp.int32, x.shape, 0)
    w = row % TW
    edge = jnp.zeros((TW, x.shape[1]), jnp.float32)
    for wi, dw in enumerate((-1, 0, 1)):
        s = x
        if dw:
            s = pltpu.roll(x, (-dw) % VOX, 0)
            s = jnp.where((w + dw >= 0) & (w + dw < TW), s, 0.0)
        for d in range(TD):
            plane = s[d * PLANE:(d + 1) * PLANE]
            odd[wi, d + 1] = plane.astype(jnp.bfloat16)
            even[wi, d + 1] = jnp.concatenate([edge, plane, edge], 0).astype(jnp.bfloat16)


def patch(even, odd, tap):
    dd, dh, dw = tap_offset(tap)
    if dh == 0:
        cut = odd[dw + 1, dd + 1:dd + 1 + TD]
    else:
        lo = (dh + 1) * TW
        cut = even[dw + 1, dd + 1:dd + 1 + TD, lo:lo + PLANE]
    return cut.reshape(VOX, cut.shape[-1])


def kernel(n, nsec, plan, incoming, feed, weights, up, grad,
           w_ref, first, pool, nxt, upv, ea, oa, eb, ob, a_send, d_send, d_mid, a_recv, d_recv, big, acc,
           w_sem, in_sem, up_sem, sec_s, sec_r, as_s, as_r, ar_s, ar_r, ap_s, ap_r,
           dz_s, dz_r, dy_s, dy_r, dm_s, dm_r, mp_s, mp_r):
    me = lax.axis_index("dp")
    sec = lax.axis_index("section")
    ny, nz = a_recv.shape[2:4]
    core = lax.rem(me, 2)
    y = lax.rem(me // 2, ny)
    z = me // (2 * ny)
    mate = me + 1 - 2 * core
    block = d_recv.shape[-2]
    half = block // 2
    last = sec == nsec - 1

    def at(zz, yy, cc):
        return (zz * ny + yy) * 2 + cc

    def z_of(k):
        low, high = lax.rem(z, 2), z // 2
        low = 1 - low if k % 2 else low
        high = 1 - high if k // 2 else high
        return 2 * high + low

    def y_of(k):
        return lax.rem(y + k, ny)

    load_in = pltpu.make_async_copy(incoming.at[0], first, in_sem.at[0])
    load_pool = pltpu.make_async_copy(feed, pool, in_sem.at[1])
    loads = [pltpu.make_async_copy(weights.at[0, b], w_ref.at[b], w_sem.at[b]) for b in (0, 1)]
    load_in.start()
    loads[1].start()
    loads[0].start()
    load_pool.start()

    barrier = pltpu.get_barrier_semaphore()
    peers = [mate]
    peers += [at(z_of(k), y, cc) for k in range(1, nz) for cc in (0, 1)]
    peers += [at(z, y_of(k), cc) for k in range(1, ny) for cc in (0, 1)]
    for peer in peers:
        pl.semaphore_signal(barrier, inc=1, device_id={"dp": peer}, device_id_type=MESH)

    @pl.when(sec > 0)
    def _():
        pl.semaphore_signal(barrier, inc=1, device_id={"section": sec - 1}, device_id_type=MESH)

    @pl.when(sec < nsec - 1)
    def _():
        pl.semaphore_signal(barrier, inc=1, device_id={"section": sec + 1}, device_id_type=MESH)

    for wi in range(3):
        for ref in (ea, oa, eb, ob):
            for d in (0, TD + 1):
                ref[wi, d] = jnp.zeros(ref.shape[2:], jnp.bfloat16)
    load_in.wait()
    extra = jnp.where(sec > 0, 1, 0) + jnp.where(sec < nsec - 1, 1, 0)
    pl.semaphore_wait(barrier, len(peers) + extra)

    def a_direct(stage, idx, peer, to, slot):
        return pltpu.make_async_remote_copy(
            src_ref=a_send.at[stage, to], dst_ref=a_recv.at[(stage, to) + slot],
            send_sem=as_s.at[stage, idx], recv_sem=as_r.at[(stage,) + slot],
            device_id={"dp": peer}, device_id_type=MESH)

    def a_relay(stage, yy, slot):
        return pltpu.make_async_remote_copy(
            src_ref=a_recv.at[(stage, core) + slot], dst_ref=a_recv.at[(stage, core) + slot],
            send_sem=ar_s.at[stage, yy, slot[1]], recv_sem=ar_r.at[(stage,) + slot],
            device_id={"dp": at(z, yy, core)}, device_id_type=MESH)

    def d_along_z(stage, zz, slot):
        return pltpu.make_async_remote_copy(
            src_ref=d_send.at[stage, zz], dst_ref=d_mid.at[stage, :, slot],
            send_sem=dz_s.at[stage, zz], recv_sem=dz_r.at[stage, slot],
            device_id={"dp": at(zz, y, core)}, device_id_type=MESH)

    def d_along_y(stage, yy, slot):
        return pltpu.make_async_remote_copy(
            src_ref=d_mid.at[stage, yy], dst_ref=d_recv.at[stage, core, slot],
            send_sem=dy_s.at[stage, yy], recv_sem=dy_r.at[stage, slot],
            device_id={"dp": at(z, yy, core)}, device_id_type=MESH)

    def d_to_mate(stage, whose):
        return pltpu.make_async_remote_copy(
            src_ref=d_recv.at[stage, whose], dst_ref=d_recv.at[stage, whose],
            send_sem=dm_s.at[stage], recv_sem=dm_r.at[stage],
            device_id={"dp": mate}, device_id_type=MESH)

    def directs(stage):
        mine = (y, z, core)
        out = []
        for k in (1, 2):
            for cc in (0, 1):
                out.append(a_direct(stage, len(out), at(z_of(k), y, cc), cc, mine))
        for k in range(1, ny):
            for cc in (0, 1):
                out.append(a_direct(stage, len(out), at(z, y_of(k), cc), cc, mine))
        out.append(a_direct(stage, len(out), mate, 1 - core, mine))
        return out

    def share(stage, act, err):
        a_send[stage, 0] = act[:, :LANES]
        a_send[stage, 1] = act[:, LANES:]
        turned = jnp.transpose(err).astype(jnp.bfloat16)
        d_send[stage] = turned.reshape(d_send.shape[1:])
        for k in range(1, nz):
            d_along_z(stage, z_of(k), z).start()
        for copy in directs(stage):
            copy.start()
        a_recv[stage, core, y, z, core] = a_send[stage, core]
        for yy in range(ny):
            d_mid[stage, yy, z] = d_send[stage, z, yy]

    def pass_on(stage, slot):
        return pltpu.make_async_remote_copy(
            src_ref=a_recv.at[stage, core, y, slot], dst_ref=a_recv.at[stage, core, y, slot],
            send_sem=ap_s.at[stage], recv_sem=ap_r.at[stage],
            device_id={"dp": at(z_of(1), y, core)}, device_id_type=MESH)

    def a_to_mate(stage, whose, yy):
        return pltpu.make_async_remote_copy(
            src_ref=a_recv.at[stage, whose, yy], dst_ref=a_recv.at[stage, whose, yy],
            send_sem=mp_s.at[stage, yy], recv_sem=mp_r.at[stage, yy],
            device_id={"dp": mate}, device_id_type=MESH)

    def relay_near(stage):
        for cc in (0, 1):
            a_direct(stage, 0, mate, 0, (y, z_of(2), cc)).wait_recv()
        pass_on(stage, z_of(2)).start()
        for j in range(1, ny):
            a_relay(stage, y_of(j), (y, z_of(2))).start()
        for cc in (0, 1):
            a_direct(stage, 0, mate, 0, (y, z_of(1), cc)).wait_recv()
        for j in range(1, ny):
            a_relay(stage, y_of(j), (y, z_of(1))).start()

    def relay_far(stage):
        for k in range(1, nz):
            d_along_z(stage, z, z_of(k)).wait_recv()
        for k in range(1, ny):
            d_along_y(stage, y_of(k), y).start()
        d_recv[stage, core, y] = d_mid[stage, y]
        pass_on(stage, z_of(3)).wait_recv()
        for j in range(1, ny):
            a_relay(stage, y_of(j), (y, z_of(3))).start()
        a_direct(stage, 0, mate, 0, (y, z, 1 - core)).wait_recv()
        a_to_mate(stage, core, y).start()

    def swap_errors(stage):
        for k in range(1, ny):
            d_along_y(stage, y, y_of(k)).wait_recv()
        d_to_mate(stage, core).start()

    def arrive(stage):
        for j in range(1, ny):
            for cc in (0, 1):
                a_direct(stage, 0, mate, 0, (y_of(j), z, cc)).wait_recv()
            for k in range(1, nz):
                a_relay(stage, y, (y_of(j), z_of(k))).wait_recv()
            a_to_mate(stage, core, y_of(j)).start()

    def mate_arrives(stage):
        for j in range(ny):
            a_to_mate(stage, 1 - core, y_of(j)).wait_recv()

    def sent(stage):
        for k in range(1, nz):
            d_along_z(stage, z_of(k), z).wait_send()
        for copy in directs(stage):
            copy.wait_send()
        for j in range(1, ny):
            d_along_y(stage, y_of(j), y).wait_send()
            for k in range(1, nz):
                a_relay(stage, y_of(j), (y, z_of(k))).wait_send()
        pass_on(stage, z_of(2)).wait_send()
        for j in range(ny):
            a_to_mate(stage, core, y_of(j)).wait_send()
        d_to_mate(stage, core).wait_send()

    def convs(b, near, far):
        near()
        fwd = jnp.zeros((VOX, w_ref.shape[2]), jnp.float32)
        for tap in range(TAPS):
            fwd += lax.dot_general(patch(ea, oa, tap), w_ref[b, tap], (((1,), (1,)), ((), ())),
                                   preferred_element_type=jnp.float32)
        far()
        bwd = jnp.zeros((VOX, w_ref.shape[3]), jnp.float32)
        for tap in range(TAPS):
            bwd += jnp.dot(patch(eb, ob, TAPS - 1 - tap), w_ref[b, tap],
                           preferred_element_type=jnp.float32)
        return fwd, bwd

    def sec_copy(j):
        return pltpu.make_async_remote_copy(
            src_ref=upv.at[0, j], dst_ref=nxt.at[j], send_sem=sec_s.at[j], recv_sem=sec_r.at[j],
            device_id={"section": lax.rem(sec + nsec - 1, nsec)}, device_id_type=MESH)

    stages = 2 * TICKS
    depth = n * VOX

    lane = lax.broadcasted_iota(jnp.int32, (8, VOX), 1)
    masks = {}
    for step, size in ((1, TW), (TW, TH), (PLANE, TD)):
        at_axis = (lane // step) % size
        masks[step] = at_axis >= 1
        masks[-step] = at_axis < size - 1

    def moved(x, by):
        if by == 0:
            return x
        return jnp.where(masks[by], pltpu.roll(x, by % VOX, 2), 0.0)

    def gradient(stage):
        b = stage % 2
        d_to_mate(stage, 1 - core).wait_recv()
        arrive(stage)

        @pl.loop(0, n // 2)
        def _(r):
            yy, zz = r // nz, lax.rem(r, nz)
            for cc in (0, 1):
                x = d_recv[stage, cc, yy, zz].astype(jnp.float32)
                x = jnp.where(core == 0, x[:half], x[half:]).reshape(half // 8, 8, VOX)
                cols = pl.ds(pl.multiple_of((2 * r + cc) * VOX, VOX), VOX)
                rows = [None] * TAPS
                for dw in (-1, 0, 1):
                    xw = moved(x, dw)
                    for dh in (-1, 0, 1):
                        xh = moved(xw, dh * TW)
                        for dd in (-1, 0, 1):
                            tap = 9 * (dd + 1) + 3 * (dh + 1) + dw + 1
                            rows[tap] = moved(xh, dd * PLANE).reshape(half, VOX)
                big[:, cols] = jnp.concatenate(rows, 0).astype(jnp.bfloat16)

        mate_arrives(stage)
        both = jnp.concatenate([a_recv[stage, 0].reshape(depth, LANES),
                                a_recv[stage, 1].reshape(depth, LANES)], 1)
        got = jnp.dot(big[...], both, preferred_element_type=jnp.float32)
        if stage < 2:
            acc[b] = got
        else:
            grad[1 - b] = (acc[b] + got).reshape(TAPS, half, 2 * LANES)

    for tick in range(TICKS):
        if tick == 0:
            cur = first
        else:
            cur = nxt
            relay_near(1)
            swap_errors(0)
            gradient(0)
            relay_far(1)
            load_pool.wait()

            @pl.when(last)
            def _():
                nxt[...] = pool[plan[0, 0]]

            @pl.when(sec < nsec - 1)
            def _():
                for j in range(4):
                    sec_copy(j).wait_recv()
        y1 = cur[0].astype(jnp.float32)
        s1 = sigmoid(y1)
        a1 = y1 * s1
        dy2 = cur[3].astype(jnp.float32)
        share(2 * tick, a1.astype(jnp.bfloat16), dy2)
        fill(ea, oa, a1)
        fill(eb, ob, dy2)
        if tick == 0:
            loads[1].wait()
        fwd, bwd = convs(1, lambda: None, lambda: None)
        x2 = (cur[1].astype(jnp.float32) - fwd).astype(jnp.bfloat16)
        dx1 = (cur[2].astype(jnp.float32) + bwd * silu_grad(y1, s1)).astype(jnp.bfloat16)
        upv[tick, 1] = x2
        upv[tick, 2] = dx1
        if tick == 0:
            @pl.when(sec > 0)
            def _():
                sec_copy(1).start()
                sec_copy(2).start()
        u = x2.astype(jnp.float32)
        s2 = sigmoid(u)
        a2 = u * s2
        e1 = dx1.astype(jnp.float32)
        share(2 * tick + 1, a2.astype(jnp.bfloat16), e1)
        fill(ea, oa, a2)
        fill(eb, ob, e1)
        if tick == 0:
            loads[0].wait()
        fwd, bwd = convs(0, lambda: relay_near(2 * tick), lambda: relay_far(2 * tick))
        u = upv[tick, 1].astype(jnp.float32)
        s2 = sigmoid(u)
        upv[tick, 0] = (cur[0].astype(jnp.float32) - fwd).astype(jnp.bfloat16)
        upv[tick, 3] = (cur[3].astype(jnp.float32) + bwd * silu_grad(u, s2)).astype(jnp.bfloat16)
        if tick == 0:
            @pl.when(sec > 0)
            def _():
                sec_copy(0).start()
                sec_copy(3).start()
        pltpu.make_async_copy(upv.at[tick], up.at[tick], up_sem.at[tick]).start()

    relay_near(stages - 1)
    swap_errors(1)
    for stage in range(1, stages):
        if stage == 2:
            relay_far(stages - 1)
        if stage + 1 < stages:
            swap_errors(stage + 1)
        gradient(stage)

    @pl.loop(0, stages)
    def _(stage):
        sent(stage)

    for tick in range(TICKS):
        pltpu.make_async_copy(upv.at[tick], up.at[tick], up_sem.at[tick]).wait()

    @pl.when(sec > 0)
    def _():
        for j in range(4):
            sec_copy(j).wait_send()


def body(incoming, feed, plan, weights, momentum):
    n = lax.axis_size("dp")
    nsec = lax.axis_size("section")
    channels = weights.shape[-1]
    block = 2 * channels // n
    ny = max(1, n // 8)
    nz = n // (2 * ny)
    stages = 2 * TICKS
    bf, f32 = jnp.bfloat16, jnp.float32
    vm = pl.BlockSpec(memory_space=pltpu.VMEM)
    hbm = pl.BlockSpec(memory_space=pl.ANY)
    dma = pltpu.SemaphoreType.DMA
    incoming = pltpu.with_memory_space_constraint(incoming, pltpu.HBM)
    feed = pltpu.with_memory_space_constraint(feed, pltpu.HBM)
    up, grad = pl.pallas_call(
        functools.partial(kernel, n, nsec),
        out_shape=(
            jax.ShapeDtypeStruct((TICKS, 4, VOX, channels), bf),
            jax.ShapeDtypeStruct((2, TAPS, block // 2, channels), f32),
        ),
        in_specs=[pl.BlockSpec(memory_space=pltpu.SMEM)] + [pl.BlockSpec(memory_space=pltpu.HBM)] * 3,
        out_specs=(hbm, vm),
        scratch_shapes=[
            pltpu.VMEM(weights.shape[1:], bf),
            pltpu.VMEM((4, VOX, channels), bf),
            pltpu.VMEM(feed.shape, bf),
            pltpu.VMEM((4, VOX, channels), bf),
            pltpu.VMEM((TICKS, 4, VOX, channels), bf),
            pltpu.VMEM((3, TD + 2, PLANE + 2 * TW, channels), bf),
            pltpu.VMEM((3, TD + 2, PLANE, channels), bf),
            pltpu.VMEM((3, TD + 2, PLANE + 2 * TW, channels), bf),
            pltpu.VMEM((3, TD + 2, PLANE, channels), bf),
            pltpu.VMEM((stages, 2, VOX, LANES), bf),
            pltpu.VMEM((stages, nz, ny, block, VOX), bf),
            pltpu.VMEM((stages, ny, nz, block, VOX), bf),
            pltpu.VMEM((stages, 2, ny, nz, 2, VOX, LANES), bf),
            pltpu.VMEM((stages, 2, ny, nz, block, VOX), bf),
            pltpu.VMEM((TAPS * block // 2, n * VOX), bf),
            pltpu.VMEM((2, TAPS * block // 2, channels), f32),
            dma((2,)), dma((2,)), dma((TICKS,)), dma((4,)), dma((4,)),
            dma((stages, 2 * (ny + nz))), dma((stages, ny, nz, 2)), dma((stages, ny, nz)), dma((stages, ny, nz)),
            dma((stages,)), dma((stages,)),
            dma((stages, nz)), dma((stages, nz)), dma((stages, ny)), dma((stages, ny)),
            dma((stages,)), dma((stages,)), dma((stages, ny)), dma((stages, ny)),
        ],
        compiler_params=pltpu.CompilerParams(
            collective_id=0, has_side_effects=True, vmem_limit_bytes=48 * 1024 * 1024),
        cost_estimate=pl.CostEstimate(flops=12 * TICKS * VOX * TAPS * channels * channels,
                                      bytes_accessed=weights.size * 2, transcendentals=0),
    )(plan, incoming, feed, weights)
    new_momentum = 0.9 * momentum[0] + grad / (n * TICKS)
    return (up[:, None], new_momentum[None])


def solution(mesh):
    in_specs = (
        P("section", None, "dp", None),
        P(None, None, "dp", None),
        P(None, "dp"),
        P("section", None, None, None, None),
        P("section", None, None, "dp", None),
    )
    out_specs = (P(None, "section", None, "dp", None), P("section", None, None, "dp", None))
    return jax.shard_map(body, mesh=mesh, in_specs=in_specs, out_specs=out_specs, check_vma=False)
```
